512 devices in a mesh: section: 2 (over core), tile: 128 (over z_lo, y, x), sub: 2 (over z_hi).
Axes of the slice: x: 4, y: 4, z: 16 (z_hi: 2, z_lo: 8; z = z_hi * 8 + z_lo), core: 2. Of those that a mesh axis runs over, the one named last changes fastest.
Arguments:
- traces: float32 [16384, 8, 1024], P(('section', 'tile', 'sub')), may hold values from -6 to 6
- band_gain: float32 [1024], replicated, may hold values from 0.2 to 2
- aperture: int32 [16384, 4], P(('section', 'tile', 'sub')), may hold values from 0 to 127, all different within a row; in each aligned block of 32 rows (0 to 31, 32 to 63, ...) at most 2 rows name the same one
- taper: float32 [16384, 4], P(('section', 'tile', 'sub')), may hold values from 0.25 to 1
- weights: float32 [128, 1024, 1536], P('tile', None, ('section', 'sub')), may hold values from -0.375 to 0.375
- spread: float32 [128, 8, 128], P('tile'), may hold values from -3 to 3
Outputs:
- image: float32 [128, 1536, 128], P('tile', ('section', 'sub'))
The draws below stay inside these ranges and needn't reach their ends.
Inputs may be any that keep to these rules, and one draw needn't show every extreme that they name: `aperture`: each row names 4 different tiles; among the 32 rows of one device no tile is named more than 2 times, a bound that some block reaches; every tile is named by some row.
All inputs are finite; a program needn't handle non-finite values.
Results may differ from the reference program's by a relative error of at most 0.000094.
Values sent between devices are 32-bit elements; how exact they have to be, the bound alone decides.
No kernel may reach another device: no remote copies, remote signals or barrier semaphores. Data moves between devices by JAX's collectives and lax.ppermute only.
A program may use at most 64 MiB of HBM per device.

```python
import math
import jax
import jax.numpy as jnp
import numpy as np
from jax import lax

NT = 1024
BT = 8
APER = 4
BLK_DEV = 32
CELLS = 128
TILES = 128
CAP = 2
BLOCKS = 16384
DEPTH = 1536


def block_scale(key, dims, split, smallest, largest):
    factor_of = 1.0
    for axis_at, parts in split:
        steps = jax.random.uniform(jax.random.fold_in(jax.random.fold_in(key, 6), axis_at), (parts,), jnp.float32, smallest / len(split), largest / len(split))
        factor_of = factor_of * jnp.repeat(jnp.exp(steps), dims[axis_at] // parts).reshape((-1,) + (1,) * (len(dims) - 1 - axis_at))
    return factor_of


def assign_block(rng, own, number, rows, count, top, limit, skew):
    ranking = jax.random.permutation(rng, count)
    heavy_load, common = shares(count, rows * top, limit, skew, True), shares(count, rows * top, limit, skew, False)
    places = jnp.arange(count)

    def named(sizes, rotation):
        used = int((sizes > 0).sum())
        fixed = max(1, used // 4)
        moved = fixed + (places - fixed + rotation * (used - fixed)) % max(1, count - fixed)
        return jnp.zeros((count,), jnp.int32).at[ranking[jnp.where(places < fixed, places, moved)]].set(jnp.asarray(sizes, jnp.int32))

    sizes = jnp.where(number % 4 == 0, named(heavy_load, number // 4), named(common, number - number // 4 - 1))
    mixed = jax.random.permutation(jax.random.fold_in(own, 3), count)
    donor, receiver = mixed[0:count // 2 * 2:2], mixed[1:count // 2 * 2:2]
    room = jnp.minimum(sizes[donor] - 1, limit - sizes[receiver]) // 2
    room = jnp.where((donor == ranking[0]) | (receiver == ranking[0]) | (sizes[receiver] == 0), 0, jnp.maximum(room, 0))
    moved = jax.random.randint(jax.random.fold_in(own, 4), (count // 2,), 0, 1 << 20) % (room + 1)
    sizes = sizes.at[donor].add(-moved).at[receiver].add(moved)
    items = jnp.searchsorted(jnp.cumsum(sizes), jnp.arange(rows * top), side="right").astype(jnp.int32)
    table = items.reshape(top, rows).T
    table = table[jax.random.permutation(jax.random.fold_in(own, 1), rows)]
    rotation = jax.random.randint(jax.random.fold_in(own, 2), (rows, 1), 0, top)
    return jnp.take_along_axis(table, (jnp.arange(top)[None, :] + rotation) % top, axis=1)


def shares(count, total, limit, skew, full):
    weights = [(1 << 20) // math.isqrt(standing ** skew) + 1 for standing in range(1, count + 1)]
    largest = limit if full else min(limit, max(-(-total // count), total * weights[0] // sum(weights)))
    least = 1 if total - largest >= count - 1 else 0
    holding, spare = [largest] + [least] * (count - 1), total - largest - least * (count - 1)
    while spare > 0:
        movable = [i for i in range(1, count) if holding[i] < largest] or [i for i in range(1, count) if holding[i] < limit]
        whole, budget = sum([weights[i] for i in movable]), spare
        for i in movable:
            more = min(limit - holding[i], max(1, budget * weights[i] // whole), spare)
            holding[i] = holding[i] + more
            spare = spare - more
    return np.array(holding)


def centred(own_key, dims, scale, limit, split=(), kind=jnp.bfloat16):
    factor_of = block_scale(own_key, dims, split, -0.22, 0.18) if split else 1.0
    array = jax.random.normal(own_key, dims, jnp.float32) * scale * factor_of
    return jnp.minimum(jnp.maximum(array, -limit), limit).astype(kind)


def setup_inputs(seed: int = 0) -> dict:
    arg_keys = jax.random.split(jax.random.key(seed), 7)
    traces = centred(arg_keys[0], (BLOCKS, BT, NT), 1.0, 6.0, ((0, 512),), jnp.float32)
    band_gain = jnp.clip(jnp.exp(jax.random.uniform(arg_keys[1], (NT,), jnp.float32, math.log(0.2), math.log(2.0))), 0.2, 2.0)
    aperture_keys = jax.random.split(jax.random.fold_in(arg_keys[2], 1), BLOCKS // BLK_DEV)
    aperture_turns = jax.random.permutation(jax.random.fold_in(arg_keys[2], 3), BLOCKS // BLK_DEV)
    aperture = jax.vmap(lambda own, number: assign_block(jax.random.fold_in(arg_keys[2], 2), own, number, BLK_DEV, TILES, APER, CAP, 2))(aperture_keys, aperture_turns).reshape((BLOCKS, APER))
    taper = jnp.clip(jnp.exp(math.log(1.0) - 1.3862944 * jax.random.uniform(arg_keys[3], (BLOCKS, APER), jnp.float32) ** block_scale(arg_keys[3], (BLOCKS, APER), ((0, 512),), -0.2, 0.2)), 0.25, 1.0)
    weights = centred(arg_keys[4], (TILES, NT, DEPTH), (NT // 4) ** -0.5, 0.375, ((0, 128), (2, 4)), jnp.float32)
    spread = centred(arg_keys[5], (TILES, BT, CELLS), (BT // 2) ** -0.5, 3.0, ((0, 128),), jnp.float32)
    return {"traces": traces, "band_gain": band_gain, "aperture": aperture, "taper": taper, "weights": weights, "spread": spread}


def reference(traces, band_gain, aperture, taper, weights, spread):
    spectra = jnp.fft.fft(traces, axis=-1)
    filtered = jnp.real(jnp.fft.ifft(spectra * band_gain, axis=-1)).astype(jnp.float32)
    tile_ids = jnp.arange(TILES, dtype=jnp.int32)
    one_hot = (aperture[:, :, None] == tile_ids[None, None, :]).astype(jnp.float32)
    mixing = lax.optimization_barrier(jnp.sum(one_hot * taper[:, :, None], axis=1))
    fold_count = lax.optimization_barrier(jnp.sum(one_hot, axis=(0, 1)))
    flat_blocks = filtered.reshape(BLOCKS, BT * NT)
    stacked = lax.dot_general(mixing, flat_blocks, (((0,), (0,)), ((), ())), precision=lax.Precision.HIGHEST, preferred_element_type=jnp.float32)
    stacked = stacked.reshape(TILES, BT, NT)
    focused = jnp.einsum('trs,tsz->trz', stacked, weights, precision=lax.Precision.HIGHEST)
    image = jnp.einsum('trz,trc->tzc', focused, spread, precision=lax.Precision.HIGHEST)
    return image / jnp.sqrt(fold_count)[:, None, None]
```

```python
import math

import jax
import jax.numpy as jnp
import numpy as np
from jax import lax
from jax.experimental import pallas as pl
from jax.experimental.pallas import tpu as pltpu
from jax.sharding import Mesh
from jax.sharding import PartitionSpec as P

LANES = 128
RADIX = 8
VMEM = pl.BlockSpec(memory_space=pltpu.VMEM)
SMEM = pl.BlockSpec(memory_space=pltpu.SMEM)
PLANE = ("section", "y", "x")
COLUMN = ("z", "sub")


def halves(value):
    high = value.astype(jnp.bfloat16)
    low = (value - high.astype(jnp.float32)).astype(jnp.bfloat16)
    return high, low


def product(left_high, left_low, right_high, right_low):
    rows = left_high.shape[0]
    both = jnp.dot(
        jnp.concatenate([left_high, left_low], axis=0),
        right_high,
        preferred_element_type=jnp.float32,
    )
    cross = jnp.dot(left_high, right_low, preferred_element_type=jnp.float32)
    return both[:rows] + (both[rows:] + cross)


def pack_kernel(rows_hbm, lists_ref, out_ref, columns_ref, sems):
    blocks = rows_hbm.shape[0] // 8
    copies = []
    for j in range(8):
        copy = pltpu.make_async_copy(
            rows_hbm.at[:, j * LANES : (j + 1) * LANES], columns_ref.at[j], sems.at[j]
        )
        copy.start()
        copies.append(copy)
    for d in range(32):
        out_ref[d, 2 * blocks :, :] = lists_ref[...]
    for j in range(8):
        copies[j].wait()
        q, h = j // 2, j % 2
        for r in range(8):
            out_ref[4 * r + q, h * blocks : (h + 1) * blocks, :] = columns_ref[
                j, pl.ds(r, blocks, stride=8), :
            ]


def stack_kernel(got_ref, out_ref):
    sources, height, _ = got_ref.shape
    blocks = (height - 8) // 2
    tiles = 128
    tile_ids = lax.broadcasted_iota(jnp.int32, (tiles, LANES), 0).astype(jnp.float32)
    mixing, naming = [], []
    for g in range(sources // 4):
        lists = got_ref[4 * g, 2 * blocks :, :]
        for i in range(1, 4):
            lists = lists + got_ref[4 * g + i, 2 * blocks :, :]
        mix = jnp.zeros((tiles, LANES), jnp.float32)
        names = jnp.zeros((tiles, LANES), jnp.float32)
        for a in range(4):
            hit = lists[a : a + 1, :] == tile_ids
            mix = mix + jnp.where(hit, lists[4 + a : 5 + a, :], 0.0)
            names = names + jnp.where(hit, 1.0, 0.0)
        mixing.append(mix)
        naming.append(names)
    mix_high, mix_low = halves(jnp.concatenate(mixing, axis=1))
    samples = jnp.concatenate(
        [
            got_ref[:, h * blocks : (h + 1) * blocks, :].reshape(sources * blocks, LANES)
            for h in range(2)
        ],
        axis=1,
    )
    stacked = product(mix_high, mix_low, *halves(samples))
    named = naming[0]
    for names in naming[1:]:
        named = named + names
    counts = lax.dot_general(
        jnp.ones((8, LANES), jnp.bfloat16),
        named.astype(jnp.bfloat16),
        (((1,), (1,)), ((), ())),
        preferred_element_type=jnp.float32,
    )
    peers = out_ref.shape[0]
    per_plane = tiles // (peers // 2)
    for p in range(peers):
        first = (p // 2) * per_plane
        for h in range(2):
            out_ref[p, pl.ds(h, per_plane, stride=2), :] = stacked[
                first : first + per_plane, h * LANES : (h + 1) * LANES
            ]
        out_ref[p, 2 * per_plane :, :] = counts


def sum_kernel(got_ref, out_ref, counts_ref):
    total = got_ref[0]
    for p in range(1, got_ref.shape[0]):
        total = total + got_ref[p]
    rows = total.shape[0] - 8
    out_ref[:rows, :] = total[:rows]
    out_ref[rows:, :] = total[:rows]
    counts_ref[...] = total[rows:]


def image_kernel(
    tile_ref,
    stacked_ref,
    counts_ref,
    gain_ref,
    turn_cos_ref,
    turn_sin_ref,
    ahead_high_ref,
    ahead_low_ref,
    back_high_ref,
    back_low_ref,
    spread_ref,
    weights_hbm,
    out_ref,
    weights_ref,
    sem,
):
    copy = pltpu.make_async_copy(weights_hbm, weights_ref, sem)
    copy.start()
    samples = RADIX * LANES
    parts = [stacked_ref[pl.ds(j, 8, stride=RADIX), :] for j in range(RADIX)]
    angle = [2.0 * math.pi * j / RADIX for j in range(RADIX)]

    def weighted(terms, factors):
        total = None
        for term, factor in zip(terms, factors):
            if abs(factor) < 1e-9:
                continue
            if abs(factor - 1.0) < 1e-9:
                piece = term
            elif abs(factor + 1.0) < 1e-9:
                piece = -term
            else:
                piece = term * np.float32(factor)
            total = piece if total is None else total + piece
        return jnp.zeros_like(terms[0]) if total is None else total

    real_rows, imag_rows = [], []
    for k in range(RADIX):
        real = weighted(parts, [math.cos(angle[j * k % RADIX]) for j in range(RADIX)])
        imag = weighted(parts, [-math.sin(angle[j * k % RADIX]) for j in range(RADIX)])
        turn_cos = turn_cos_ref[k : k + 1, :]
        turn_sin = turn_sin_ref[k : k + 1, :]
        real_rows.append(real * turn_cos + imag * turn_sin)
        imag_rows.append(imag * turn_cos - real * turn_sin)
    waves = jnp.concatenate(
        [jnp.concatenate(real_rows, axis=0), jnp.concatenate(imag_rows, axis=0)], axis=1
    )
    spectra = product(*halves(waves), ahead_high_ref[...], ahead_low_ref[...])
    gains = jnp.concatenate(
        [jnp.broadcast_to(gain_ref[k : k + 1, :], (8, LANES)) for k in range(RADIX)], axis=0
    )
    spectra = spectra * jnp.concatenate([gains, gains], axis=1)
    waves = product(*halves(spectra), back_high_ref[...], back_low_ref[...])
    real_rows, imag_rows = [], []
    for k in range(RADIX):
        real = waves[8 * k : 8 * k + 8, :LANES]
        imag = waves[8 * k : 8 * k + 8, LANES:]
        turn_cos = turn_cos_ref[k : k + 1, :]
        turn_sin = turn_sin_ref[k : k + 1, :]
        real_rows.append(real * turn_cos - imag * turn_sin)
        imag_rows.append(imag * turn_cos + real * turn_sin)
    filtered = []
    for j in range(RADIX):
        filtered.append(
            weighted(
                real_rows + imag_rows,
                [math.cos(angle[j * k % RADIX]) for k in range(RADIX)]
                + [-math.sin(angle[j * k % RADIX]) for k in range(RADIX)],
            )
            * np.float32(1.0 / samples)
        )
    filtered = jnp.concatenate(filtered, axis=1)
    lane = lax.broadcasted_iota(jnp.int32, (1, LANES), 1)
    fold = jnp.sum(
        jnp.where(lane == tile_ref[0], counts_ref[0:1, :], 0.0), axis=1, keepdims=True
    )
    copy.wait()
    focused = product(*halves(filtered), *halves(weights_ref[...])) / jnp.sqrt(fold)
    focused_high, focused_low = halves(focused)
    spread_high, spread_low = halves(spread_ref[...])
    out_ref[...] = lax.dot_general(
        jnp.concatenate([focused_high, focused_high, focused_low], axis=0),
        jnp.concatenate([spread_high, spread_low, spread_high], axis=0),
        (((0,), (0,)), ((), ())),
        preferred_element_type=jnp.float32,
    )


def fourier_parts():
    lane = np.arange(LANES)
    turns = 2.0 * np.pi * np.arange(RADIX)[:, None] * lane[None, :] / (RADIX * LANES)
    angles = 2.0 * np.pi * (lane[:, None] * lane[None, :] % LANES) / LANES
    cosine, sine = np.cos(angles), np.sin(angles)
    ahead = np.block([[cosine, -sine], [sine, cosine]]).astype(np.float32)
    ahead_high = ahead.astype(jnp.bfloat16)
    ahead_low = (ahead - ahead_high.astype(np.float32)).astype(jnp.bfloat16)
    return (
        np.cos(turns).astype(np.float32),
        np.sin(turns).astype(np.float32),
        ahead_high,
        ahead_low,
        np.ascontiguousarray(ahead_high.T),
        np.ascontiguousarray(ahead_low.T),
    )


def body(traces, band_gain, aperture, taper, weights, spread):
    f32 = jnp.float32
    blocks, per_block, samples = traces.shape
    x_at = lax.axis_index("x")
    tile_at = (lax.axis_index("z") * 4 + lax.axis_index("y")) * 4 + x_at
    lists = jnp.concatenate([aperture.astype(f32).T, taper.T], axis=0)
    owner = jnp.arange(LANES, dtype=jnp.int32) // blocks
    lists = jnp.where((owner == x_at)[None, :], jnp.tile(lists, (1, LANES // blocks)), 0.0)
    sent = pl.pallas_call(
        pack_kernel,
        out_shape=jax.ShapeDtypeStruct((32, 2 * blocks + 8, LANES), f32),
        in_specs=[pl.BlockSpec(memory_space=pl.ANY), VMEM],
        out_specs=VMEM,
        scratch_shapes=[
            pltpu.VMEM((8, blocks * per_block, LANES), f32),
            pltpu.SemaphoreType.DMA((8,)),
        ],
        name="pack",
    )(traces.reshape(blocks * per_block, samples), lists)
    got = lax.all_to_all(sent, PLANE, 0, 0, tiled=True)
    sent = pl.pallas_call(
        stack_kernel,
        out_shape=jax.ShapeDtypeStruct((16, 40, LANES), f32),
        in_specs=[VMEM],
        out_specs=VMEM,
        name="stack",
    )(got)
    got = lax.all_to_all(sent, COLUMN, 0, 0, tiled=True)
    sent, counts = pl.pallas_call(
        sum_kernel,
        out_shape=(
            jax.ShapeDtypeStruct((64, LANES), f32),
            jax.ShapeDtypeStruct((8, LANES), f32),
        ),
        in_specs=[VMEM],
        out_specs=(VMEM, VMEM),
        name="sum",
    )(got)
    got = lax.all_to_all(sent.reshape(32, 2, LANES), PLANE, 0, 0, tiled=True)
    depth = weights.shape[2]
    image = pl.pallas_call(
        image_kernel,
        out_shape=jax.ShapeDtypeStruct((depth, spread.shape[2]), f32),
        in_specs=[SMEM] + [VMEM] * 10 + [pl.BlockSpec(memory_space=pl.ANY)],
        out_specs=VMEM,
        scratch_shapes=[pltpu.VMEM((samples, depth), f32), pltpu.SemaphoreType.DMA],
        name="image",
    )(
        tile_at.astype(jnp.int32).reshape(1),
        got.reshape(64, LANES),
        counts,
        band_gain.reshape(LANES, RADIX).T,
        *[jnp.asarray(part) for part in fourier_parts()],
        spread[0],
        weights[0],
    )
    return image[None]


def solution(mesh):
    fine = Mesh(mesh.devices.reshape(2, 8, 4, 4, 2), ("section", "z", "y", "x", "sub"))
    tile = ("z", "y", "x")
    everyone = ("section",) + tile + ("sub",)
    placed = (
        P(everyone, None, None),
        P(),
        P(everyone, None),
        P(everyone, None),
        P(tile, None, ("section", "sub")),
        P(tile, None, None),
    )
    return jax.shard_map(
        body,
        mesh=fine,
        in_specs=placed,
        out_specs=P(tile, ("section", "sub"), None),
        check_vma=False,
    )
```

```python
import math

import jax
import jax.numpy as jnp
import numpy as np
from jax import lax
from jax.experimental import pallas as pl
from jax.experimental.pallas import tpu as pltpu
from jax.sharding import Mesh
from jax.sharding import PartitionSpec as P

LANES = 128
RADIX = 8
VMEM = pl.BlockSpec(memory_space=pltpu.VMEM)
SMEM = pl.BlockSpec(memory_space=pltpu.SMEM)
NEAR = ("section", "z_pair", "y", "x")
FAR = ("z_far", "sub")
MIB = 1 << 20


def halves(value):
    high = value.astype(jnp.bfloat16)
    low = (value - high.astype(jnp.float32)).astype(jnp.bfloat16)
    return high, low


def product(left_high, left_low, right_high, right_low):
    rows = left_high.shape[0]
    both = jnp.dot(
        jnp.concatenate([left_high, left_low], axis=0),
        right_high,
        preferred_element_type=jnp.float32,
    )
    cross = jnp.dot(left_high, right_low, preferred_element_type=jnp.float32)
    return both[:rows] + (both[rows:] + cross)


def pack_kernel(x_ref, rows_hbm, aperture_ref, taper_ref, out_ref, columns_ref, sems):
    blocks = rows_hbm.shape[0] // 8
    copies = []
    for j in range(8):
        copy = pltpu.make_async_copy(
            rows_hbm.at[:, j * LANES : (j + 1) * LANES], columns_ref.at[j], sems.at[j]
        )
        copy.start()
        copies.append(copy)
    lists = jnp.concatenate([aperture_ref[...].astype(jnp.float32), taper_ref[...]], axis=0)
    lists = jnp.concatenate([lists] * (LANES // blocks), axis=1)
    owner = lax.broadcasted_iota(jnp.int32, (8, LANES), 1) // blocks
    lists = jnp.where(owner == x_ref[0], lists, 0.0)
    for d in range(64):
        out_ref[d, blocks:, :] = lists
    for j in range(8):
        copies[j].wait()
        for r in range(8):
            out_ref[8 * r + j, :blocks, :] = columns_ref[j, pl.ds(r, blocks, stride=8), :]


def stack_kernel(got_ref, out_ref):
    sources, height, _ = got_ref.shape
    blocks = height - 8
    tiles = 128
    tile_ids = lax.broadcasted_iota(jnp.int32, (tiles, LANES), 0).astype(jnp.float32)
    mixing, named = [], jnp.zeros((tiles, LANES), jnp.float32)
    for g in range(sources // 4):
        lists = got_ref[4 * g, blocks:, :]
        for i in range(1, 4):
            lists = lists + got_ref[4 * g + i, blocks:, :]
        mix = jnp.zeros((tiles, LANES), jnp.float32)
        for a in range(4):
            hit = lists[a : a + 1, :] == tile_ids
            mix = jnp.where(hit, lists[4 + a : 5 + a, :], mix)
        mixing.append(mix)
        named = named + jnp.where(mix > 0.0, 1.0, 0.0)
    mix_high, mix_low = halves(jnp.concatenate(mixing, axis=1))
    samples = got_ref[:, :blocks, :].reshape(sources * blocks, LANES)
    stacked = product(mix_high, mix_low, *halves(samples))
    counts = lax.dot_general(
        jnp.ones((8, LANES), jnp.bfloat16),
        named.astype(jnp.bfloat16),
        (((1,), (1,)), ((), ())),
        preferred_element_type=jnp.float32,
    )
    for p in range(out_ref.shape[0]):
        first = (p // 2) * 32
        out_ref[p, :32, :] = stacked[first : first + 32]
        out_ref[p, 32:, :] = counts


def sum_kernel(got_ref, out_ref, counts_ref):
    total = got_ref[0]
    for p in range(1, got_ref.shape[0]):
        total = total + got_ref[p]
    out_ref[:32, :] = total[:32]
    out_ref[32:, :] = total[:32]
    counts_ref[...] = total[32:]


def image_kernel(
    tile_ref,
    stacked_ref,
    counts_ref,
    gain_ref,
    turn_cos_ref,
    turn_sin_ref,
    table_ref,
    spread_ref,
    weights_hbm,
    out_ref,
    weights_ref,
    sem,
):
    copy = pltpu.make_async_copy(weights_hbm, weights_ref, sem)
    copy.start()
    samples = RADIX * LANES
    parts = [stacked_ref[pl.ds(j, 8, stride=RADIX), :] for j in range(RADIX)]
    angle = [2.0 * math.pi * j / RADIX for j in range(RADIX)]

    def weighted(terms, factors):
        total = None
        for term, factor in zip(terms, factors):
            if abs(factor) < 1e-9:
                continue
            if abs(factor - 1.0) < 1e-9:
                piece = term
            elif abs(factor + 1.0) < 1e-9:
                piece = -term
            else:
                piece = term * np.float32(factor)
            total = piece if total is None else total + piece
        return jnp.zeros_like(terms[0]) if total is None else total

    real_rows, imag_rows = [], []
    for k in range(RADIX):
        real = weighted(parts, [math.cos(angle[j * k % RADIX]) for j in range(RADIX)])
        imag = weighted(parts, [-math.sin(angle[j * k % RADIX]) for j in range(RADIX)])
        turn_cos = turn_cos_ref[k : k + 1, :]
        turn_sin = turn_sin_ref[k : k + 1, :]
        real_rows.append(real * turn_cos + imag * turn_sin)
        imag_rows.append(imag * turn_cos - real * turn_sin)
    waves = jnp.concatenate(
        [jnp.concatenate(real_rows, axis=0), jnp.concatenate(imag_rows, axis=0)], axis=1
    )
    ahead = halves(table_ref[...])
    back = []
    for part in ahead:
        top = jnp.concatenate([part[:LANES, :LANES], part[LANES:, :LANES]], axis=1)
        bottom = jnp.concatenate([part[:LANES, LANES:], part[LANES:, LANES:]], axis=1)
        back.append(jnp.concatenate([top, bottom], axis=0))
    spectra = product(*halves(waves), *ahead)
    gains = jnp.concatenate(
        [jnp.broadcast_to(gain_ref[k : k + 1, :], (8, LANES)) for k in range(RADIX)], axis=0
    )
    spectra = spectra * jnp.concatenate([gains, gains], axis=1)
    waves = product(*halves(spectra), *back)
    real_rows, imag_rows = [], []
    for k in range(RADIX):
        real = waves[8 * k : 8 * k + 8, :LANES]
        imag = waves[8 * k : 8 * k + 8, LANES:]
        turn_cos = turn_cos_ref[k : k + 1, :]
        turn_sin = turn_sin_ref[k : k + 1, :]
        real_rows.append(real * turn_cos - imag * turn_sin)
        imag_rows.append(imag * turn_cos + real * turn_sin)
    filtered = []
    for j in range(RADIX):
        filtered.append(
            weighted(
                real_rows + imag_rows,
                [math.cos(angle[j * k % RADIX]) for k in range(RADIX)]
                + [-math.sin(angle[j * k % RADIX]) for k in range(RADIX)],
            )
            * np.float32(1.0 / samples)
        )
    filtered = jnp.concatenate(filtered, axis=1)
    lane = lax.broadcasted_iota(jnp.int32, (1, LANES), 1)
    fold = jnp.sum(
        jnp.where(lane == tile_ref[0], counts_ref[0:1, :], 0.0), axis=1, keepdims=True
    )
    copy.wait()
    focused = product(*halves(filtered), *halves(weights_ref[...])) / jnp.sqrt(fold)
    focused_high, focused_low = halves(focused)
    spread_high, spread_low = halves(spread_ref[...])
    out_ref[...] = lax.dot_general(
        jnp.concatenate([focused_high, focused_high, focused_low], axis=0),
        jnp.concatenate([spread_high, spread_low, spread_high], axis=0),
        (((0,), (0,)), ((), ())),
        preferred_element_type=jnp.float32,
    )


def fourier_parts():
    lane = np.arange(LANES)
    turns = 2.0 * np.pi * np.arange(RADIX)[:, None] * lane[None, :] / (RADIX * LANES)
    angles = 2.0 * np.pi * (lane[:, None] * lane[None, :] % LANES) / LANES
    cosine, sine = np.cos(angles), np.sin(angles)
    return (
        np.cos(turns).astype(np.float32),
        np.sin(turns).astype(np.float32),
        np.block([[cosine, -sine], [sine, cosine]]).astype(np.float32),
    )


def body(traces, band_gain, aperture, taper, weights, spread):
    f32 = jnp.float32
    blocks, per_block, samples = traces.shape
    depth = weights.shape[2]
    x_at = lax.axis_index("x")
    z_at = lax.axis_index("z_far") * 2 + lax.axis_index("z_pair")
    tile_at = (z_at * 4 + lax.axis_index("y")) * 4 + x_at
    sent = pl.pallas_call(
        pack_kernel,
        out_shape=jax.ShapeDtypeStruct((64, blocks + 8, LANES), f32),
        in_specs=[SMEM, pl.BlockSpec(memory_space=pltpu.HBM), VMEM, VMEM],
        out_specs=VMEM,
        scratch_shapes=[
            pltpu.VMEM((8, blocks * per_block, LANES), f32),
            pltpu.SemaphoreType.DMA((8,)),
        ],
        compiler_params=pltpu.CompilerParams(vmem_limit_bytes=6 * MIB),
        name="pack",
    )(x_at.reshape(1), traces.reshape(blocks * per_block, samples), aperture.T, taper.T)
    got = lax.all_to_all(sent, NEAR, 0, 0, tiled=True)
    sent = pl.pallas_call(
        stack_kernel,
        out_shape=jax.ShapeDtypeStruct((8, 40, LANES), f32),
        in_specs=[VMEM],
        out_specs=VMEM,
        compiler_params=pltpu.CompilerParams(vmem_limit_bytes=16 * MIB),
        name="stack",
    )(got)
    got = lax.all_to_all(sent, FAR, 0, 0, tiled=True)
    sent, counts = pl.pallas_call(
        sum_kernel,
        out_shape=(
            jax.ShapeDtypeStruct((64, LANES), f32),
            jax.ShapeDtypeStruct((8, LANES), f32),
        ),
        in_specs=[VMEM],
        out_specs=(VMEM, VMEM),
        compiler_params=pltpu.CompilerParams(vmem_limit_bytes=2 * MIB),
        name="sum",
    )(got)
    got = lax.all_to_all(sent.reshape(64, 1, LANES), NEAR, 0, 0, tiled=True)
    image = pl.pallas_call(
        image_kernel,
        out_shape=jax.ShapeDtypeStruct((depth, spread.shape[2]), f32),
        in_specs=[SMEM] + [VMEM] * 7 + [pl.BlockSpec(memory_space=pl.ANY)],
        out_specs=VMEM,
        scratch_shapes=[pltpu.VMEM((samples, depth), f32), pltpu.SemaphoreType.DMA],
        compiler_params=pltpu.CompilerParams(vmem_limit_bytes=16 * MIB),
        name="image",
    )(
        tile_at.reshape(1),
        got.reshape(64, LANES),
        counts,
        band_gain.reshape(LANES, RADIX).T,
        *[jnp.asarray(part) for part in fourier_parts()],
        spread[0],
        weights[0],
    )
    return image[None]


def solution(mesh):
    fine = Mesh(
        mesh.devices.reshape(2, 4, 2, 4, 4, 2),
        ("section", "z_far", "z_pair", "y", "x", "sub"),
    )
    tile = ("z_far", "z_pair", "y", "x")
    everyone = ("section",) + tile + ("sub",)
    placed = (
        P(everyone, None, None),
        P(),
        P(everyone, None),
        P(everyone, None),
        P(tile, None, ("section", "sub")),
        P(tile, None, None),
    )
    return jax.shard_map(
        body,
        mesh=fine,
        in_specs=placed,
        out_specs=P(tile, ("section", "sub"), None),
        check_vma=False,
    )
```

```python
import math

import jax
import jax.numpy as jnp
import numpy as np
from jax import lax
from jax.experimental import pallas as pl
from jax.experimental.pallas import tpu as pltpu
from jax.sharding import Mesh
from jax.sharding import PartitionSpec as P

LANES = 128
RADIX = 8
VMEM = pl.BlockSpec(memory_space=pltpu.VMEM)
SMEM = pl.BlockSpec(memory_space=pltpu.SMEM)
NEAR = ("section", "z_pair", "y", "x")
FAR = ("z_far", "sub")
MIB = 1 << 20


def halves(value):
    high = value.astype(jnp.bfloat16)
    low = (value - high.astype(jnp.float32)).astype(jnp.bfloat16)
    return high, low


def product(left_high, left_low, right_high, right_low):
    rows = left_high.shape[0]
    both = jnp.dot(
        jnp.concatenate([left_high, left_low], axis=0),
        right_high,
        preferred_element_type=jnp.float32,
    )
    cross = jnp.dot(left_high, right_low, preferred_element_type=jnp.float32)
    return both[:rows] + (both[rows:] + cross)


def pack_kernel(x_ref, rows_hbm, lists_ref, out_ref, columns_ref, sems):
    blocks = rows_hbm.shape[0] // 8
    copies = []
    for j in range(8):
        copy = pltpu.make_async_copy(
            rows_hbm.at[:, j * LANES : (j + 1) * LANES], columns_ref.at[j], sems.at[j]
        )
        copy.start()
        copies.append(copy)
    lists = jnp.concatenate([lists_ref[0], lists_ref[1]], axis=0)
    lists = jnp.concatenate([lists] * 4, axis=1)
    entry = lax.broadcasted_iota(jnp.int32, (8, LANES), 0) + x_ref[0]
    lane = lax.broadcasted_iota(jnp.int32, (8, LANES), 1)
    lists = jnp.where(lane // blocks == entry % 4, lists, 0.0)
    lists = jnp.concatenate(
        [jnp.sum(lists[4 * i : 4 * i + 4], axis=0, keepdims=True) for i in range(2)], axis=0
    )
    height = blocks + 2
    for d in range(64):
        out_ref[height * d + blocks : height * (d + 1), :] = lists
    for j in range(8):
        copies[j].wait()
        for r in range(8):
            first = height * (8 * r + j)
            out_ref[first : first + blocks, :] = columns_ref[j, pl.ds(r, blocks, stride=8), :]


def stack_kernel(got_ref, out_ref):
    sources, blocks, tiles = 64, 32, 128
    height = blocks + 2
    tile_ids = lax.broadcasted_iota(jnp.int32, (tiles, LANES), 0).astype(jnp.float32)
    row = lax.broadcasted_iota(jnp.int32, (8, LANES), 0)
    lane = lax.broadcasted_iota(jnp.int32, (8, LANES), 1)
    own = lane // blocks == row % 4

    def entries(offset, first, a):
        rows = got_ref[pl.ds(height * first + offset, 8, stride=height), :]
        rows = rows if a == 0 else pltpu.roll(rows, LANES - blocks * a, axis=1)
        rows = jnp.where(own, rows, 0.0)
        rows = rows + pltpu.roll(rows, 1, axis=0)
        return rows + pltpu.roll(rows, 2, axis=0)

    mixing, named = [], jnp.zeros((tiles, LANES), jnp.float32)
    for first in range(0, sources, 8):
        apertures = [entries(blocks, first, a) for a in range(4)]
        tapers = [entries(blocks + 1, first, a) for a in range(4)]
        for at in (3, 7):
            mix = jnp.zeros((tiles, LANES), jnp.float32)
            for a in range(4):
                hit = apertures[a][at : at + 1, :] == tile_ids
                mix = jnp.where(hit, tapers[a][at : at + 1, :], mix)
            mixing.append(mix)
            named = named + jnp.where(mix > 0.0, 1.0, 0.0)
    mix_high, mix_low = halves(jnp.concatenate(mixing, axis=1))
    samples = jnp.concatenate(
        [got_ref[height * s : height * s + blocks, :] for s in range(sources)], axis=0
    )
    stacked = product(mix_high, mix_low, *halves(samples))
    counts = lax.dot_general(
        jnp.ones((8, LANES), jnp.bfloat16),
        named.astype(jnp.bfloat16),
        (((1,), (1,)), ((), ())),
        preferred_element_type=jnp.float32,
    )
    for p in range(8):
        first = (p // 2) * 32
        out_ref[33 * p : 33 * p + 32, :] = stacked[first : first + 32]
        out_ref[33 * p + 32 : 33 * p + 33, :] = counts[:1]


def sum_kernel(got_ref, out_ref, counts_ref):
    total, counts = got_ref[:32, :], got_ref[32:33, :]
    for p in range(1, 8):
        total = total + got_ref[33 * p : 33 * p + 32, :]
        counts = counts + got_ref[33 * p + 32 : 33 * p + 33, :]
    out_ref[:32, :] = total
    out_ref[32:, :] = total
    counts_ref[...] = counts


def image_kernel(
    tile_ref,
    stacked_ref,
    counts_ref,
    gain_ref,
    turn_cos_ref,
    turn_sin_ref,
    table_ref,
    spread_ref,
    weights_hbm,
    out_ref,
    weights_ref,
    sem,
):
    copy = pltpu.make_async_copy(weights_hbm, weights_ref, sem)
    copy.start()
    samples = RADIX * LANES
    parts = [stacked_ref[pl.ds(j, 8, stride=RADIX), :] for j in range(RADIX)]
    angle = [2.0 * math.pi * j / RADIX for j in range(RADIX)]

    def weighted(terms, factors):
        total = None
        for term, factor in zip(terms, factors):
            if abs(factor) < 1e-9:
                continue
            if abs(factor - 1.0) < 1e-9:
                piece = term
            elif abs(factor + 1.0) < 1e-9:
                piece = -term
            else:
                piece = term * np.float32(factor)
            total = piece if total is None else total + piece
        return jnp.zeros_like(terms[0]) if total is None else total

    real_rows, imag_rows = [], []
    for k in range(RADIX):
        real = weighted(parts, [math.cos(angle[j * k % RADIX]) for j in range(RADIX)])
        imag = weighted(parts, [-math.sin(angle[j * k % RADIX]) for j in range(RADIX)])
        turn_cos = turn_cos_ref[k : k + 1, :]
        turn_sin = turn_sin_ref[k : k + 1, :]
        real_rows.append(real * turn_cos + imag * turn_sin)
        imag_rows.append(imag * turn_cos - real * turn_sin)
    waves = jnp.concatenate(
        [jnp.concatenate(real_rows, axis=0), jnp.concatenate(imag_rows, axis=0)], axis=1
    )
    ahead = halves(table_ref[...])
    back = []
    for part in ahead:
        top = jnp.concatenate([part[:LANES, :LANES], part[LANES:, :LANES]], axis=1)
        bottom = jnp.concatenate([part[:LANES, LANES:], part[LANES:, LANES:]], axis=1)
        back.append(jnp.concatenate([top, bottom], axis=0))
    spectra = product(*halves(waves), *ahead)
    gains = jnp.concatenate(
        [jnp.broadcast_to(gain_ref[k : k + 1, :], (8, LANES)) for k in range(RADIX)], axis=0
    )
    spectra = spectra * jnp.concatenate([gains, gains], axis=1)
    waves = product(*halves(spectra), *back)
    real_rows, imag_rows = [], []
    for k in range(RADIX):
        real = waves[8 * k : 8 * k + 8, :LANES]
        imag = waves[8 * k : 8 * k + 8, LANES:]
        turn_cos = turn_cos_ref[k : k + 1, :]
        turn_sin = turn_sin_ref[k : k + 1, :]
        real_rows.append(real * turn_cos - imag * turn_sin)
        imag_rows.append(imag * turn_cos + real * turn_sin)
    filtered = []
    for j in range(RADIX):
        filtered.append(
            weighted(
                real_rows + imag_rows,
                [math.cos(angle[j * k % RADIX]) for k in range(RADIX)]
                + [-math.sin(angle[j * k % RADIX]) for k in range(RADIX)],
            )
            * np.float32(1.0 / samples)
        )
    filtered = jnp.concatenate(filtered, axis=1)
    lane = lax.broadcasted_iota(jnp.int32, (1, LANES), 1)
    fold = jnp.sum(
        jnp.where(lane == tile_ref[0], counts_ref[0:1, :], 0.0), axis=1, keepdims=True
    )
    copy.wait()
    focused = product(*halves(filtered), *halves(weights_ref[...])) / jnp.sqrt(fold)
    focused_high, focused_low = halves(focused)
    spread_high, spread_low = halves(spread_ref[...])
    out_ref[...] = lax.dot_general(
        jnp.concatenate([focused_high, focused_high, focused_low], axis=0),
        jnp.concatenate([spread_high, spread_low, spread_high], axis=0),
        (((0,), (0,)), ((), ())),
        preferred_element_type=jnp.float32,
    )


def fourier_parts():
    lane = np.arange(LANES)
    turns = 2.0 * np.pi * np.arange(RADIX)[:, None] * lane[None, :] / (RADIX * LANES)
    angles = 2.0 * np.pi * (lane[:, None] * lane[None, :] % LANES) / LANES
    cosine, sine = np.cos(angles), np.sin(angles)
    return (
        np.cos(turns).astype(np.float32),
        np.sin(turns).astype(np.float32),
        np.block([[cosine, -sine], [sine, cosine]]).astype(np.float32),
    )


def body(traces, band_gain, aperture, taper, weights, spread):
    f32 = jnp.float32
    blocks, per_block, samples = traces.shape
    depth = weights.shape[2]
    x_at = lax.axis_index("x")
    z_at = lax.axis_index("z_far") * 2 + lax.axis_index("z_pair")
    tile_at = (z_at * 4 + lax.axis_index("y")) * 4 + x_at
    lists = jnp.where(
        jnp.arange(2)[:, None, None] == 0, aperture.T.astype(f32)[None], taper.T[None]
    )
    sent = pl.pallas_call(
        pack_kernel,
        out_shape=jax.ShapeDtypeStruct((64 * (blocks + 2), LANES), f32),
        in_specs=[SMEM, pl.BlockSpec(memory_space=pl.ANY), VMEM],
        out_specs=VMEM,
        scratch_shapes=[
            pltpu.VMEM((8, blocks * per_block, LANES), f32),
            pltpu.SemaphoreType.DMA((8,)),
        ],
        compiler_params=pltpu.CompilerParams(vmem_limit_bytes=6 * MIB),
        name="pack",
    )(x_at.reshape(1), traces.reshape(blocks * per_block, samples), lists)
    got = lax.all_to_all(sent.reshape(64, -1, 2, LANES), NEAR, 0, 0, tiled=True)
    sent = pl.pallas_call(
        stack_kernel,
        out_shape=jax.ShapeDtypeStruct((8 * 33, LANES), f32),
        in_specs=[VMEM],
        out_specs=VMEM,
        compiler_params=pltpu.CompilerParams(vmem_limit_bytes=16 * MIB),
        name="stack",
    )(got.reshape(-1, LANES))
    got = lax.all_to_all(sent.reshape(8, 33, 1, LANES), FAR, 0, 0, tiled=True)
    sent, counts = pl.pallas_call(
        sum_kernel,
        out_shape=(
            jax.ShapeDtypeStruct((64, LANES), f32),
            jax.ShapeDtypeStruct((1, LANES), f32),
        ),
        in_specs=[VMEM],
        out_specs=(VMEM, VMEM),
        compiler_params=pltpu.CompilerParams(vmem_limit_bytes=2 * MIB),
        name="sum",
    )(got.reshape(-1, LANES))
    got = lax.all_to_all(sent.reshape(64, 1, LANES), NEAR, 0, 0, tiled=True)
    image = pl.pallas_call(
        image_kernel,
        out_shape=jax.ShapeDtypeStruct((depth, spread.shape[2]), f32),
        in_specs=[SMEM] + [VMEM] * 7 + [pl.BlockSpec(memory_space=pl.ANY)],
        out_specs=VMEM,
        scratch_shapes=[pltpu.VMEM((samples, depth), f32), pltpu.SemaphoreType.DMA],
        compiler_params=pltpu.CompilerParams(vmem_limit_bytes=16 * MIB),
        name="image",
    )(
        tile_at.reshape(1),
        got.reshape(64, LANES),
        counts,
        band_gain.reshape(LANES, RADIX).T,
        *[jnp.asarray(part) for part in fourier_parts()],
        spread[0],
        weights[0],
    )
    return image[None]


def solution(mesh):
    fine = Mesh(
        mesh.devices.reshape(2, 4, 2, 4, 4, 2),
        ("section", "z_far", "z_pair", "y", "x", "sub"),
    )
    tile = ("z_far", "z_pair", "y", "x")
    everyone = ("section",) + tile + ("sub",)
    placed = (
        P(everyone, None, None),
        P(),
        P(everyone, None),
        P(everyone, None),
        P(tile, None, ("section", "sub")),
        P(tile, None, None),
    )
    return jax.shard_map(
        body,
        mesh=fine,
        in_specs=placed,
        out_specs=P(tile, ("section", "sub"), None),
        check_vma=False,
    )
```

```python
import math

import jax
import jax.numpy as jnp
import numpy as np
from jax import lax
from jax.experimental import pallas as pl
from jax.experimental.pallas import tpu as pltpu
from jax.sharding import Mesh
from jax.sharding import PartitionSpec as P

LANES = 128
RADIX = 8
HBM = pl.BlockSpec(memory_space=pl.ANY)
VMEM = pl.BlockSpec(memory_space=pltpu.VMEM)
SMEM = pl.BlockSpec(memory_space=pltpu.SMEM)
NEAR = ("section", "y", "x", "z_pair")
SPREAD_FIRST = 63
GATHER_FIRST = 63
SPREAD_ORDER = [(SPREAD_FIRST + i) % 64 for i in range(64)]
GATHER_ORDER = [(GATHER_FIRST + i) % 64 for i in range(64)]
FAR = ("z_far", "sub")
FAR_ORDER = [1, 0, 3, 2, 5, 4, 7, 6]
TILE = ("z_far", "z_pair", "y", "x")
SIZES = {"section": 2, "z_pair": 2, "y": 4, "x": 4}
MIB = 1 << 20


def halves(value):
    high = value.astype(jnp.bfloat16)
    low = (value - high.astype(jnp.float32)).astype(jnp.bfloat16)
    return high, low


def product(left_high, left_low, right_high, right_low):
    rows = left_high.shape[0]
    both = jnp.dot(
        jnp.concatenate([left_high, left_low], axis=0),
        right_high,
        preferred_element_type=jnp.float32,
    )
    cross = jnp.dot(left_high, right_low, preferred_element_type=jnp.float32)
    return both[:rows] + (both[rows:] + cross)


def in_hbm(array):
    return pltpu.with_memory_space_constraint(array, pltpu.HBM)


def pack_kernel(
    place_ref,
    rows_hbm,
    aperture_hbm,
    taper_hbm,
    out_ref,
    columns_ref,
    aperture_ref,
    taper_ref,
    sems,
    list_sems,
):
    blocks = rows_hbm.shape[0] // 8
    copies = [
        pltpu.make_async_copy(aperture_hbm, aperture_ref, list_sems.at[0]),
        pltpu.make_async_copy(taper_hbm, taper_ref, list_sems.at[1]),
    ]
    for copy in copies:
        copy.start()
    for j in range(8):
        copy = pltpu.make_async_copy(
            rows_hbm.at[:, j * LANES : (j + 1) * LANES], columns_ref.at[j], sems.at[j]
        )
        copy.start()
        copies.append(copy)
    copies.pop(0).wait()
    copies.pop(0).wait()
    lists = jnp.concatenate([aperture_ref[...].astype(jnp.float32), taper_ref[...]], axis=0)
    lists = jnp.concatenate([lists] * 4, axis=1)
    entry = lax.broadcasted_iota(jnp.int32, (8, LANES), 0) + place_ref[0]
    lane = lax.broadcasted_iota(jnp.int32, (8, LANES), 1)
    lists = jnp.where(lane // blocks == entry % 4, lists, 0.0)
    lists = jnp.concatenate(
        [jnp.sum(lists[4 * i : 4 * i + 4], axis=0, keepdims=True) for i in range(2)], axis=0
    )
    height = blocks + 2
    for d in range(64):
        out_ref[height * d + blocks : height * (d + 1), :] = lists
    for j in range(8):
        copies[j].wait()
        for r in range(8):
            first = height * SPREAD_ORDER.index(GATHER_ORDER[8 * r + j])
            out_ref[first : first + blocks, :] = columns_ref[j, pl.ds(r, blocks, stride=8), :]


def stack_kernel(got_ref, out_ref):
    sources, blocks, tiles = 64, 32, 128
    height = blocks + 2
    tile_ids = lax.broadcasted_iota(jnp.int32, (tiles, LANES), 0).astype(jnp.float32)
    row = lax.broadcasted_iota(jnp.int32, (8, LANES), 0)
    lane = lax.broadcasted_iota(jnp.int32, (8, LANES), 1)
    own = lane // blocks == row % 4

    def entries(offset, first, a):
        rows = got_ref[pl.ds(height * first + offset, 8, stride=height), :]
        rows = rows if a == 0 else pltpu.roll(rows, LANES - blocks * a, axis=1)
        rows = jnp.where(own, rows, 0.0)
        rows = rows + pltpu.roll(rows, 1, axis=0)
        return rows + pltpu.roll(rows, 2, axis=0)

    mixing, named = [], jnp.zeros((tiles, LANES), jnp.float32)
    for first in range(0, sources, 8):
        apertures = [entries(blocks, first, a) for a in range(4)]
        tapers = [entries(blocks + 1, first, a) for a in range(4)]
        for at in (3, 7):
            mix = jnp.zeros((tiles, LANES), jnp.float32)
            for a in range(4):
                hit = apertures[a][at : at + 1, :] == tile_ids
                mix = jnp.where(hit, tapers[a][at : at + 1, :], mix)
            mixing.append(mix)
            named = named + jnp.where(mix > 0.0, 1.0, 0.0)
    mix_high, mix_low = halves(jnp.concatenate(mixing, axis=1))
    samples = jnp.concatenate(
        [got_ref[height * s : height * s + blocks, :] for s in range(sources)], axis=0
    )
    stacked = product(mix_high, mix_low, *halves(samples))
    counts = lax.dot_general(
        jnp.ones((8, LANES), jnp.bfloat16),
        named.astype(jnp.bfloat16),
        (((1,), (1,)), ((), ())),
        preferred_element_type=jnp.float32,
    )
    for p in range(8):
        first = (FAR_ORDER[p] // 2) * 32
        out_ref[33 * p : 33 * p + 32, :] = stacked[first : first + 32]
        out_ref[33 * p + 32 : 33 * p + 33, :] = counts[:1]


def near_tiles():
    owners = []
    places = list(np.ndindex(*[SIZES[axis] for axis in NEAR]))
    for index in GATHER_ORDER:
        at = dict(zip(NEAR, places[index]))
        owners.append((at["z_pair"] * 4 + at["y"]) * 4 + at["x"])
    return owners


def sum_kernel(got_ref, out_ref, counts_ref):
    total, counts = got_ref[:32, :], got_ref[32:33, :]
    for p in range(1, 8):
        total = total + got_ref[33 * p : 33 * p + 32, :]
        counts = counts + got_ref[33 * p + 32 : 33 * p + 33, :]
    for d, owner in enumerate(near_tiles()):
        out_ref[d : d + 1, :] = total[owner : owner + 1]
    counts_ref[...] = counts


def image_kernel(
    tile_ref,
    stacked_ref,
    counts_ref,
    gain_ref,
    turn_cos_ref,
    turn_sin_ref,
    table_ref,
    spread_ref,
    weights_hbm,
    out_ref,
    weights_ref,
    sem,
):
    copy = pltpu.make_async_copy(weights_hbm, weights_ref, sem)
    copy.start()
    samples = RADIX * LANES
    parts = [stacked_ref[pl.ds(j, 8, stride=RADIX), :] for j in range(RADIX)]
    angle = [2.0 * math.pi * j / RADIX for j in range(RADIX)]

    def weighted(terms, factors):
        total = None
        for term, factor in zip(terms, factors):
            if abs(factor) < 1e-9:
                continue
            if abs(factor - 1.0) < 1e-9:
                piece = term
            elif abs(factor + 1.0) < 1e-9:
                piece = -term
            else:
                piece = term * np.float32(factor)
            total = piece if total is None else total + piece
        return jnp.zeros_like(terms[0]) if total is None else total

    real_rows, imag_rows = [], []
    for k in range(RADIX):
        real = weighted(parts, [math.cos(angle[j * k % RADIX]) for j in range(RADIX)])
        imag = weighted(parts, [-math.sin(angle[j * k % RADIX]) for j in range(RADIX)])
        turn_cos = turn_cos_ref[k : k + 1, :]
        turn_sin = turn_sin_ref[k : k + 1, :]
        real_rows.append(real * turn_cos + imag * turn_sin)
        imag_rows.append(imag * turn_cos - real * turn_sin)
    waves = jnp.concatenate(
        [jnp.concatenate(real_rows, axis=0), jnp.concatenate(imag_rows, axis=0)], axis=1
    )
    ahead = halves(table_ref[...])
    back = []
    for part in ahead:
        top = jnp.concatenate([part[:LANES, :LANES], part[LANES:, :LANES]], axis=1)
        bottom = jnp.concatenate([part[:LANES, LANES:], part[LANES:, LANES:]], axis=1)
        back.append(jnp.concatenate([top, bottom], axis=0))
    spectra = product(*halves(waves), *ahead)
    gains = jnp.concatenate(
        [jnp.broadcast_to(gain_ref[k : k + 1, :], (8, LANES)) for k in range(RADIX)], axis=0
    )
    spectra = spectra * jnp.concatenate([gains, gains], axis=1)
    waves = product(*halves(spectra), *back)
    real_rows, imag_rows = [], []
    for k in range(RADIX):
        real = waves[8 * k : 8 * k + 8, :LANES]
        imag = waves[8 * k : 8 * k + 8, LANES:]
        turn_cos = turn_cos_ref[k : k + 1, :]
        turn_sin = turn_sin_ref[k : k + 1, :]
        real_rows.append(real * turn_cos - imag * turn_sin)
        imag_rows.append(imag * turn_cos + real * turn_sin)
    filtered = []
    for j in range(RADIX):
        filtered.append(
            weighted(
                real_rows + imag_rows,
                [math.cos(angle[j * k % RADIX]) for k in range(RADIX)]
                + [-math.sin(angle[j * k % RADIX]) for k in range(RADIX)],
            )
            * np.float32(1.0 / samples)
        )
    filtered = jnp.concatenate(filtered, axis=1)
    lane = lax.broadcasted_iota(jnp.int32, (1, LANES), 1)
    fold = jnp.sum(
        jnp.where(lane == tile_ref[0], counts_ref[0:1, :], 0.0), axis=1, keepdims=True
    )
    copy.wait()
    focused = product(*halves(filtered), *halves(weights_ref[...])) / jnp.sqrt(fold)
    focused_high, focused_low = halves(focused)
    spread_high, spread_low = halves(spread_ref[...])
    out_ref[...] = lax.dot_general(
        jnp.concatenate([focused_high, focused_high, focused_low], axis=0),
        jnp.concatenate([spread_high, spread_low, spread_high], axis=0),
        (((0,), (0,)), ((), ())),
        preferred_element_type=jnp.float32,
    )


def fourier_parts():
    lane = np.arange(LANES)
    turns = 2.0 * np.pi * np.arange(RADIX)[:, None] * lane[None, :] / (RADIX * LANES)
    angles = 2.0 * np.pi * (lane[:, None] * lane[None, :] % LANES) / LANES
    cosine, sine = np.cos(angles), np.sin(angles)
    return (
        np.cos(turns).astype(np.float32),
        np.sin(turns).astype(np.float32),
        np.block([[cosine, -sine], [sine, cosine]]).astype(np.float32),
    )


def body(traces, band_gain, aperture, taper, weights, spread):
    f32 = jnp.float32
    blocks, per_block, samples = traces.shape
    depth = weights.shape[2]
    tile_at = lax.axis_index(TILE)
    sent = pl.pallas_call(
        pack_kernel,
        out_shape=jax.ShapeDtypeStruct((64 * (blocks + 2), LANES), f32),
        in_specs=[SMEM, HBM, HBM, HBM],
        out_specs=VMEM,
        scratch_shapes=[
            pltpu.VMEM((8, blocks * per_block, LANES), f32),
            pltpu.VMEM((4, blocks), jnp.int32),
            pltpu.VMEM((4, blocks), f32),
            pltpu.SemaphoreType.DMA((8,)),
            pltpu.SemaphoreType.DMA((2,)),
        ],
        compiler_params=pltpu.CompilerParams(vmem_limit_bytes=6 * MIB),
        name="pack",
    )(
        ((lax.axis_index(NEAR) - SPREAD_FIRST) % 4).reshape(1),
        in_hbm(traces.reshape(blocks * per_block, samples)),
        in_hbm(aperture.T),
        in_hbm(taper.T),
    )
    got = lax.all_to_all(
        sent.reshape(64, -1, 2, LANES), NEAR, 0, 0, axis_index_groups=[SPREAD_ORDER], tiled=True
    )
    sent = pl.pallas_call(
        stack_kernel,
        out_shape=jax.ShapeDtypeStruct((8 * 33, LANES), f32),
        in_specs=[VMEM],
        out_specs=VMEM,
        compiler_params=pltpu.CompilerParams(vmem_limit_bytes=16 * MIB),
        name="stack",
    )(got.reshape(-1, LANES))
    got = lax.all_to_all(
        sent.reshape(8, 33, 1, LANES), FAR, 0, 0, axis_index_groups=[FAR_ORDER], tiled=True
    )
    sent, counts = pl.pallas_call(
        sum_kernel,
        out_shape=(
            jax.ShapeDtypeStruct((64, LANES), f32),
            jax.ShapeDtypeStruct((1, LANES), f32),
        ),
        in_specs=[VMEM],
        out_specs=(VMEM, VMEM),
        compiler_params=pltpu.CompilerParams(vmem_limit_bytes=2 * MIB),
        name="sum",
    )(got.reshape(-1, LANES))
    got = lax.all_to_all(
        sent.reshape(64, 1, LANES), NEAR, 0, 0, axis_index_groups=[GATHER_ORDER], tiled=True
    )
    image = pl.pallas_call(
        image_kernel,
        out_shape=jax.ShapeDtypeStruct((depth, spread.shape[2]), f32),
        in_specs=[SMEM] + [VMEM] * 7 + [pl.BlockSpec(memory_space=pl.ANY)],
        out_specs=VMEM,
        scratch_shapes=[pltpu.VMEM((samples, depth), f32), pltpu.SemaphoreType.DMA],
        compiler_params=pltpu.CompilerParams(vmem_limit_bytes=16 * MIB),
        name="image",
    )(
        tile_at.reshape(1),
        got.reshape(64, LANES),
        counts,
        band_gain.reshape(LANES, RADIX).T,
        *[jnp.asarray(part) for part in fourier_parts()],
        spread[0],
        weights[0],
    )
    return image[None]


def solution(mesh):
    fine = Mesh(
        mesh.devices.reshape(2, 4, 2, 4, 4, 2),
        ("section", "z_far", "z_pair", "y", "x", "sub"),
    )
    everyone = ("section",) + TILE + ("sub",)
    placed = (
        P(everyone, None, None),
        P(),
        P(everyone, None),
        P(everyone, None),
        P(TILE, None, ("section", "sub")),
        P(TILE, None, None),
    )
    return jax.shard_map(
        body,
        mesh=fine,
        in_specs=placed,
        out_specs=P(TILE, ("section", "sub"), None),
        check_vma=False,
    )
```

```python
import math

import jax
import jax.numpy as jnp
import numpy as np
from jax import lax
from jax.experimental import pallas as pl
from jax.experimental.pallas import tpu as pltpu
from jax.sharding import Mesh
from jax.sharding import PartitionSpec as P

LANES = 128
RADIX = 8
HBM = pl.BlockSpec(memory_space=pl.ANY)
VMEM = pl.BlockSpec(memory_space=pltpu.VMEM)
SMEM = pl.BlockSpec(memory_space=pltpu.SMEM)
NEAR = ("section", "y", "x", "z_pair")
SPREAD_FIRST = 63
GATHER_FIRST = 63
SPREAD_ORDER = [(SPREAD_FIRST + i) % 64 for i in range(64)]
GATHER_ORDER = [(GATHER_FIRST + i) % 64 for i in range(64)]
FAR = ("z_far", "sub")
FAR_ORDER = [1, 0, 2, 4, 6, 7, 5, 3]
TILE = ("z_far", "z_pair", "y", "x")
SIZES = {"section": 2, "z_pair": 2, "y": 4, "x": 4}
MIB = 1 << 20


def halves(value):
    high = value.astype(jnp.bfloat16)
    low = (value - high.astype(jnp.float32)).astype(jnp.bfloat16)
    return high, low


def product(left_high, left_low, right_high, right_low):
    rows = left_high.shape[0]
    both = jnp.dot(
        jnp.concatenate([left_high, left_low], axis=0),
        right_high,
        preferred_element_type=jnp.float32,
    )
    cross = jnp.dot(left_high, right_low, preferred_element_type=jnp.float32)
    return both[:rows] + (both[rows:] + cross)


def in_hbm(array):
    return pltpu.with_memory_space_constraint(array, pltpu.HBM)


def pack_kernel(
    place_ref,
    rows_hbm,
    aperture_hbm,
    taper_hbm,
    out_ref,
    columns_ref,
    aperture_ref,
    taper_ref,
    sems,
    list_sems,
):
    blocks = rows_hbm.shape[0] // 8
    copies = [
        pltpu.make_async_copy(aperture_hbm, aperture_ref, list_sems.at[0]),
        pltpu.make_async_copy(taper_hbm, taper_ref, list_sems.at[1]),
    ]
    for copy in copies:
        copy.start()
    for j in range(8):
        copy = pltpu.make_async_copy(
            rows_hbm.at[:, j * LANES : (j + 1) * LANES], columns_ref.at[j], sems.at[j]
        )
        copy.start()
        copies.append(copy)
    copies.pop(0).wait()
    copies.pop(0).wait()
    lists = jnp.concatenate([aperture_ref[...].astype(jnp.float32), taper_ref[...]], axis=0)
    lists = jnp.concatenate([lists] * 4, axis=1)
    entry = lax.broadcasted_iota(jnp.int32, (8, LANES), 0) + place_ref[0]
    lane = lax.broadcasted_iota(jnp.int32, (8, LANES), 1)
    lists = jnp.where(lane // blocks == entry % 4, lists, 0.0)
    lists = jnp.concatenate(
        [jnp.sum(lists[4 * i : 4 * i + 4], axis=0, keepdims=True) for i in range(2)], axis=0
    )
    height = blocks + 2
    for d in range(64):
        out_ref[height * d + blocks : height * (d + 1), :] = lists
    for j in range(8):
        copies[j].wait()
        for r in range(8):
            first = height * SPREAD_ORDER.index(GATHER_ORDER[8 * r + j])
            out_ref[first : first + blocks, :] = columns_ref[j, pl.ds(r, blocks, stride=8), :]


def stack_kernel(got_ref, out_ref):
    sources, blocks, tiles = 64, 32, 128
    height = blocks + 2
    tile_ids = lax.broadcasted_iota(jnp.int32, (tiles, LANES), 0).astype(jnp.float32)
    row = lax.broadcasted_iota(jnp.int32, (8, LANES), 0)
    lane = lax.broadcasted_iota(jnp.int32, (8, LANES), 1)
    own = lane // blocks == row % 4

    def entries(offset, first, a):
        rows = got_ref[pl.ds(height * first + offset, 8, stride=height), :]
        rows = rows if a == 0 else pltpu.roll(rows, LANES - blocks * a, axis=1)
        rows = jnp.where(own, rows, 0.0)
        rows = rows + pltpu.roll(rows, 1, axis=0)
        return rows + pltpu.roll(rows, 2, axis=0)

    mixing, named = [], jnp.zeros((tiles, LANES), jnp.float32)
    for first in range(0, sources, 8):
        apertures = [entries(blocks, first, a) for a in range(4)]
        tapers = [entries(blocks + 1, first, a) for a in range(4)]
        for at in (3, 7):
            mix = jnp.zeros((tiles, LANES), jnp.float32)
            for a in range(4):
                hit = apertures[a][at : at + 1, :] == tile_ids
                mix = jnp.where(hit, tapers[a][at : at + 1, :], mix)
            mixing.append(mix)
            named = named + jnp.where(mix > 0.0, 1.0, 0.0)
    mix_high, mix_low = halves(jnp.concatenate(mixing, axis=1))
    samples = jnp.concatenate(
        [got_ref[height * s : height * s + blocks, :] for s in range(sources)], axis=0
    )
    stacked = product(mix_high, mix_low, *halves(samples))
    counts = lax.dot_general(
        jnp.ones((8, LANES), jnp.bfloat16),
        named.astype(jnp.bfloat16),
        (((1,), (1,)), ((), ())),
        preferred_element_type=jnp.float32,
    )
    for p in range(8):
        first = (FAR_ORDER[p] // 2) * 32
        out_ref[33 * p : 33 * p + 32, :] = stacked[first : first + 32]
        out_ref[33 * p + 32 : 33 * p + 33, :] = counts[:1]


def near_tiles():
    owners = []
    places = list(np.ndindex(*[SIZES[axis] for axis in NEAR]))
    for index in GATHER_ORDER:
        at = dict(zip(NEAR, places[index]))
        owners.append((at["z_pair"] * 4 + at["y"]) * 4 + at["x"])
    return owners


def sum_kernel(got_ref, out_ref, counts_ref):
    total, counts = got_ref[:32, :], got_ref[32:33, :]
    for p in range(1, 8):
        total = total + got_ref[33 * p : 33 * p + 32, :]
        counts = counts + got_ref[33 * p + 32 : 33 * p + 33, :]
    for d, owner in enumerate(near_tiles()):
        out_ref[d : d + 1, :] = total[owner : owner + 1]
    counts_ref[...] = counts


def image_kernel(
    tile_ref,
    stacked_ref,
    counts_ref,
    gain_ref,
    turn_cos_ref,
    turn_sin_ref,
    table_ref,
    spread_ref,
    weights_hbm,
    out_ref,
    weights_ref,
    sem,
):
    copy = pltpu.make_async_copy(weights_hbm, weights_ref, sem)
    copy.start()
    samples = RADIX * LANES
    parts = [stacked_ref[pl.ds(j, 8, stride=RADIX), :] for j in range(RADIX)]
    angle = [2.0 * math.pi * j / RADIX for j in range(RADIX)]

    def weighted(terms, factors):
        total = None
        for term, factor in zip(terms, factors):
            if abs(factor) < 1e-9:
                continue
            if abs(factor - 1.0) < 1e-9:
                piece = term
            elif abs(factor + 1.0) < 1e-9:
                piece = -term
            else:
                piece = term * np.float32(factor)
            total = piece if total is None else total + piece
        return jnp.zeros_like(terms[0]) if total is None else total

    real_rows, imag_rows = [], []
    for k in range(RADIX):
        real = weighted(parts, [math.cos(angle[j * k % RADIX]) for j in range(RADIX)])
        imag = weighted(parts, [-math.sin(angle[j * k % RADIX]) for j in range(RADIX)])
        turn_cos = turn_cos_ref[k : k + 1, :]
        turn_sin = turn_sin_ref[k : k + 1, :]
        real_rows.append(real * turn_cos + imag * turn_sin)
        imag_rows.append(imag * turn_cos - real * turn_sin)
    waves = jnp.concatenate(
        [jnp.concatenate(real_rows, axis=0), jnp.concatenate(imag_rows, axis=0)], axis=1
    )
    ahead = halves(table_ref[...])
    back = []
    for part in ahead:
        top = jnp.concatenate([part[:LANES, :LANES], part[LANES:, :LANES]], axis=1)
        bottom = jnp.concatenate([part[:LANES, LANES:], part[LANES:, LANES:]], axis=1)
        back.append(jnp.concatenate([top, bottom], axis=0))
    spectra = product(*halves(waves), *ahead)
    gains = jnp.concatenate(
        [jnp.broadcast_to(gain_ref[k : k + 1, :], (8, LANES)) for k in range(RADIX)], axis=0
    )
    spectra = spectra * jnp.concatenate([gains, gains], axis=1)
    waves = product(*halves(spectra), *back)
    real_rows, imag_rows = [], []
    for k in range(RADIX):
        real = waves[8 * k : 8 * k + 8, :LANES]
        imag = waves[8 * k : 8 * k + 8, LANES:]
        turn_cos = turn_cos_ref[k : k + 1, :]
        turn_sin = turn_sin_ref[k : k + 1, :]
        real_rows.append(real * turn_cos - imag * turn_sin)
        imag_rows.append(imag * turn_cos + real * turn_sin)
    filtered = []
    for j in range(RADIX):
        filtered.append(
            weighted(
                real_rows + imag_rows,
                [math.cos(angle[j * k % RADIX]) for k in range(RADIX)]
                + [-math.sin(angle[j * k % RADIX]) for k in range(RADIX)],
            )
            * np.float32(1.0 / samples)
        )
    filtered = jnp.concatenate(filtered, axis=1)
    lane = lax.broadcasted_iota(jnp.int32, (1, LANES), 1)
    fold = jnp.sum(
        jnp.where(lane == tile_ref[0], counts_ref[0:1, :], 0.0), axis=1, keepdims=True
    )
    copy.wait()
    focused = product(*halves(filtered), *halves(weights_ref[...])) / jnp.sqrt(fold)
    focused_high, focused_low = halves(focused)
    spread_high, spread_low = halves(spread_ref[...])
    out_ref[...] = lax.dot_general(
        jnp.concatenate([focused_high, focused_high, focused_low], axis=0),
        jnp.concatenate([spread_high, spread_low, spread_high], axis=0),
        (((0,), (0,)), ((), ())),
        preferred_element_type=jnp.float32,
    )


def fourier_parts():
    lane = np.arange(LANES)
    turns = 2.0 * np.pi * np.arange(RADIX)[:, None] * lane[None, :] / (RADIX * LANES)
    angles = 2.0 * np.pi * (lane[:, None] * lane[None, :] % LANES) / LANES
    cosine, sine = np.cos(angles), np.sin(angles)
    return (
        np.cos(turns).astype(np.float32),
        np.sin(turns).astype(np.float32),
        np.block([[cosine, -sine], [sine, cosine]]).astype(np.float32),
    )


def body(traces, band_gain, aperture, taper, weights, spread):
    f32 = jnp.float32
    blocks, per_block, samples = traces.shape
    depth = weights.shape[2]
    tile_at = lax.axis_index(TILE)
    sent = pl.pallas_call(
        pack_kernel,
        out_shape=jax.ShapeDtypeStruct((64 * (blocks + 2), LANES), f32),
        in_specs=[SMEM, HBM, HBM, HBM],
        out_specs=VMEM,
        scratch_shapes=[
            pltpu.VMEM((8, blocks * per_block, LANES), f32),
            pltpu.VMEM((4, blocks), jnp.int32),
            pltpu.VMEM((4, blocks), f32),
            pltpu.SemaphoreType.DMA((8,)),
            pltpu.SemaphoreType.DMA((2,)),
        ],
        compiler_params=pltpu.CompilerParams(vmem_limit_bytes=6 * MIB),
        name="pack",
    )(
        ((lax.axis_index(NEAR) - SPREAD_FIRST) % 4).reshape(1),
        in_hbm(traces.reshape(blocks * per_block, samples)),
        in_hbm(aperture.T),
        in_hbm(taper.T),
    )
    got = lax.all_to_all(
        sent.reshape(64, -1, 2, LANES), NEAR, 0, 0, axis_index_groups=[SPREAD_ORDER], tiled=True
    )
    sent = pl.pallas_call(
        stack_kernel,
        out_shape=jax.ShapeDtypeStruct((8 * 33, LANES), f32),
        in_specs=[VMEM],
        out_specs=VMEM,
        compiler_params=pltpu.CompilerParams(vmem_limit_bytes=16 * MIB),
        name="stack",
    )(got.reshape(-1, LANES))
    got = lax.all_to_all(
        sent.reshape(8, 33, 1, LANES), FAR, 0, 0, axis_index_groups=[FAR_ORDER], tiled=True
    )
    sent, counts = pl.pallas_call(
        sum_kernel,
        out_shape=(
            jax.ShapeDtypeStruct((64, LANES), f32),
            jax.ShapeDtypeStruct((1, LANES), f32),
        ),
        in_specs=[VMEM],
        out_specs=(VMEM, VMEM),
        compiler_params=pltpu.CompilerParams(vmem_limit_bytes=2 * MIB),
        name="sum",
    )(got.reshape(-1, LANES))
    got = lax.all_to_all(
        sent.reshape(64, 1, LANES), NEAR, 0, 0, axis_index_groups=[GATHER_ORDER], tiled=True
    )
    image = pl.pallas_call(
        image_kernel,
        out_shape=jax.ShapeDtypeStruct((depth, spread.shape[2]), f32),
        in_specs=[SMEM] + [VMEM] * 7 + [pl.BlockSpec(memory_space=pl.ANY)],
        out_specs=VMEM,
        scratch_shapes=[pltpu.VMEM((samples, depth), f32), pltpu.SemaphoreType.DMA],
        compiler_params=pltpu.CompilerParams(vmem_limit_bytes=16 * MIB),
        name="image",
    )(
        tile_at.reshape(1),
        got.reshape(64, LANES),
        counts,
        band_gain.reshape(LANES, RADIX).T,
        *[jnp.asarray(part) for part in fourier_parts()],
        spread[0],
        weights[0],
    )
    return image[None]


def solution(mesh):
    fine = Mesh(
        mesh.devices.reshape(2, 4, 2, 4, 4, 2),
        ("section", "z_far", "z_pair", "y", "x", "sub"),
    )
    everyone = ("section",) + TILE + ("sub",)
    placed = (
        P(everyone, None, None),
        P(),
        P(everyone, None),
        P(everyone, None),
        P(TILE, None, ("section", "sub")),
        P(TILE, None, None),
    )
    return jax.shard_map(
        body,
        mesh=fine,
        in_specs=placed,
        out_specs=P(TILE, ("section", "sub"), None),
        check_vma=False,
    )
```

```python
import math

import jax
import jax.numpy as jnp
import numpy as np
from jax import lax
from jax.experimental import pallas as pl
from jax.experimental.pallas import tpu as pltpu
from jax.sharding import Mesh
from jax.sharding import PartitionSpec as P

LANES = 128
RADIX = 8
HBM = pl.BlockSpec(memory_space=pl.ANY)
VMEM = pl.BlockSpec(memory_space=pltpu.VMEM)
SMEM = pl.BlockSpec(memory_space=pltpu.SMEM)
NEAR = ("section", "y", "x", "z_pair")
SPREAD_FIRST = 53
GATHER_FIRST = 63
SPREAD_ORDER = [(SPREAD_FIRST + i) % 64 for i in range(64)]
GATHER_ORDER = [(GATHER_FIRST + i) % 64 for i in range(64)]
FAR = ("z_far", "sub")
FAR_ORDER = [1, 0, 3, 2, 5, 4, 7, 6]
TILE = ("z_far", "z_pair", "y", "x")
SIZES = {"section": 2, "z_pair": 2, "y": 4, "x": 4}
MIB = 1 << 20


def halves(value):
    high = value.astype(jnp.bfloat16)
    low = (value - high.astype(jnp.float32)).astype(jnp.bfloat16)
    return high, low


def product(left_high, left_low, right_high, right_low):
    rows = left_high.shape[0]
    both = jnp.dot(
        jnp.concatenate([left_high, left_low], axis=0),
        right_high,
        preferred_element_type=jnp.float32,
    )
    cross = jnp.dot(left_high, right_low, preferred_element_type=jnp.float32)
    return both[:rows] + (both[rows:] + cross)


def in_hbm(array):
    return pltpu.with_memory_space_constraint(array, pltpu.HBM)


def in_vmem(array):
    return pltpu.with_memory_space_constraint(array, pltpu.VMEM)


def pack_kernel(
    place_ref,
    rows_hbm,
    aperture_hbm,
    taper_hbm,
    out_ref,
    columns_ref,
    aperture_ref,
    taper_ref,
    sems,
    list_sems,
):
    blocks = rows_hbm.shape[0] // 8
    copies = [
        pltpu.make_async_copy(aperture_hbm, aperture_ref, list_sems.at[0]),
        pltpu.make_async_copy(taper_hbm, taper_ref, list_sems.at[1]),
    ]
    for copy in copies:
        copy.start()
    for j in range(8):
        copy = pltpu.make_async_copy(
            rows_hbm.at[:, j * LANES : (j + 1) * LANES], columns_ref.at[j], sems.at[j]
        )
        copy.start()
        copies.append(copy)
    copies.pop(0).wait()
    copies.pop(0).wait()
    lists = jnp.concatenate([aperture_ref[...].astype(jnp.float32), taper_ref[...]], axis=0)
    lists = jnp.concatenate([lists] * 4, axis=1)
    entry = lax.broadcasted_iota(jnp.int32, (8, LANES), 0) + place_ref[0]
    lane = lax.broadcasted_iota(jnp.int32, (8, LANES), 1)
    lists = jnp.where(lane // blocks == entry % 4, lists, 0.0)
    lists = jnp.concatenate(
        [jnp.sum(lists[4 * i : 4 * i + 4], axis=0, keepdims=True) for i in range(2)], axis=0
    )
    height = blocks + 2
    for d in range(64):
        out_ref[height * d + blocks : height * (d + 1), :] = lists
    for j in range(8):
        copies[j].wait()
        for r in range(8):
            first = height * SPREAD_ORDER.index(GATHER_ORDER[8 * r + j])
            out_ref[first : first + blocks, :] = columns_ref[j, pl.ds(r, blocks, stride=8), :]


def stack_kernel(got_ref, out_ref):
    sources, blocks, tiles = 64, 32, 128
    height = blocks + 2
    tile_ids = lax.broadcasted_iota(jnp.int32, (tiles, LANES), 0).astype(jnp.float32)
    row = lax.broadcasted_iota(jnp.int32, (8, LANES), 0)
    lane = lax.broadcasted_iota(jnp.int32, (8, LANES), 1)
    own = lane // blocks == row % 4

    def entries(offset, first, a):
        rows = got_ref[pl.ds(height * first + offset, 8, stride=height), :]
        rows = rows if a == 0 else pltpu.roll(rows, LANES - blocks * a, axis=1)
        rows = jnp.where(own, rows, 0.0)
        rows = rows + pltpu.roll(rows, 1, axis=0)
        return rows + pltpu.roll(rows, 2, axis=0)

    mixing, named = [], jnp.zeros((tiles, LANES), jnp.float32)
    for first in range(0, sources, 8):
        apertures = [entries(blocks, first, a) for a in range(4)]
        tapers = [entries(blocks + 1, first, a) for a in range(4)]
        for at in (3, 7):
            mix = jnp.zeros((tiles, LANES), jnp.float32)
            for a in range(4):
                hit = apertures[a][at : at + 1, :] == tile_ids
                mix = jnp.where(hit, tapers[a][at : at + 1, :], mix)
            mixing.append(mix)
            named = named + jnp.where(mix > 0.0, 1.0, 0.0)
    mix_high, mix_low = halves(jnp.concatenate(mixing, axis=1))
    samples = jnp.concatenate(
        [got_ref[height * s : height * s + blocks, :] for s in range(sources)], axis=0
    )
    stacked = product(mix_high, mix_low, *halves(samples))
    counts = lax.dot_general(
        jnp.ones((8, LANES), jnp.bfloat16),
        named.astype(jnp.bfloat16),
        (((1,), (1,)), ((), ())),
        preferred_element_type=jnp.float32,
    )
    for p in range(8):
        first = (FAR_ORDER[p] // 2) * 32
        out_ref[33 * p : 33 * p + 32, :] = stacked[first : first + 32]
        out_ref[33 * p + 32 : 33 * p + 33, :] = counts[:1]


def near_tiles():
    owners = []
    places = list(np.ndindex(*[SIZES[axis] for axis in NEAR]))
    for index in GATHER_ORDER:
        at = dict(zip(NEAR, places[index]))
        owners.append((at["z_pair"] * 4 + at["y"]) * 4 + at["x"])
    return owners


def sum_kernel(got_ref, out_ref, counts_ref):
    total, counts = got_ref[:32, :], got_ref[32:33, :]
    for p in range(1, 8):
        total = total + got_ref[33 * p : 33 * p + 32, :]
        counts = counts + got_ref[33 * p + 32 : 33 * p + 33, :]
    for d, owner in enumerate(near_tiles()):
        out_ref[d : d + 1, :] = total[owner : owner + 1]
    counts_ref[...] = counts


def image_kernel(
    tile_ref,
    stacked_ref,
    counts_ref,
    gain_ref,
    turn_cos_ref,
    turn_sin_ref,
    table_ref,
    spread_ref,
    weights_ref,
    out_ref,
):
    samples = RADIX * LANES
    parts = [stacked_ref[pl.ds(j, 8, stride=RADIX), :] for j in range(RADIX)]
    angle = [2.0 * math.pi * j / RADIX for j in range(RADIX)]

    def weighted(terms, factors):
        total = None
        for term, factor in zip(terms, factors):
            if abs(factor) < 1e-9:
                continue
            if abs(factor - 1.0) < 1e-9:
                piece = term
            elif abs(factor + 1.0) < 1e-9:
                piece = -term
            else:
                piece = term * np.float32(factor)
            total = piece if total is None else total + piece
        return jnp.zeros_like(terms[0]) if total is None else total

    real_rows, imag_rows = [], []
    for k in range(RADIX):
        real = weighted(parts, [math.cos(angle[j * k % RADIX]) for j in range(RADIX)])
        imag = weighted(parts, [-math.sin(angle[j * k % RADIX]) for j in range(RADIX)])
        turn_cos = turn_cos_ref[k : k + 1, :]
        turn_sin = turn_sin_ref[k : k + 1, :]
        real_rows.append(real * turn_cos + imag * turn_sin)
        imag_rows.append(imag * turn_cos - real * turn_sin)
    waves = jnp.concatenate(
        [jnp.concatenate(real_rows, axis=0), jnp.concatenate(imag_rows, axis=0)], axis=1
    )
    ahead = halves(table_ref[...])
    back = []
    for part in ahead:
        top = jnp.concatenate([part[:LANES, :LANES], part[LANES:, :LANES]], axis=1)
        bottom = jnp.concatenate([part[:LANES, LANES:], part[LANES:, LANES:]], axis=1)
        back.append(jnp.concatenate([top, bottom], axis=0))
    spectra = product(*halves(waves), *ahead)
    gains = jnp.concatenate(
        [jnp.broadcast_to(gain_ref[k : k + 1, :], (8, LANES)) for k in range(RADIX)], axis=0
    )
    spectra = spectra * jnp.concatenate([gains, gains], axis=1)
    waves = product(*halves(spectra), *back)
    real_rows, imag_rows = [], []
    for k in range(RADIX):
        real = waves[8 * k : 8 * k + 8, :LANES]
        imag = waves[8 * k : 8 * k + 8, LANES:]
        turn_cos = turn_cos_ref[k : k + 1, :]
        turn_sin = turn_sin_ref[k : k + 1, :]
        real_rows.append(real * turn_cos - imag * turn_sin)
        imag_rows.append(imag * turn_cos + real * turn_sin)
    filtered = []
    for j in range(RADIX):
        filtered.append(
            weighted(
                real_rows + imag_rows,
                [math.cos(angle[j * k % RADIX]) for k in range(RADIX)]
                + [-math.sin(angle[j * k % RADIX]) for k in range(RADIX)],
            )
            * np.float32(1.0 / samples)
        )
    filtered = jnp.concatenate(filtered, axis=1)
    lane = lax.broadcasted_iota(jnp.int32, (1, LANES), 1)
    fold = jnp.sum(
        jnp.where(lane == tile_ref[0], counts_ref[0:1, :], 0.0), axis=1, keepdims=True
    )
    focused = product(*halves(filtered), *halves(weights_ref[...])) / jnp.sqrt(fold)
    focused_high, focused_low = halves(focused)
    spread_high, spread_low = halves(spread_ref[...])
    out_ref[...] = lax.dot_general(
        jnp.concatenate([focused_high, focused_high, focused_low], axis=0),
        jnp.concatenate([spread_high, spread_low, spread_high], axis=0),
        (((0,), (0,)), ((), ())),
        preferred_element_type=jnp.float32,
    )


def fourier_parts():
    lane = np.arange(LANES)
    turns = 2.0 * np.pi * np.arange(RADIX)[:, None] * lane[None, :] / (RADIX * LANES)
    angles = 2.0 * np.pi * (lane[:, None] * lane[None, :] % LANES) / LANES
    cosine, sine = np.cos(angles), np.sin(angles)
    return (
        np.cos(turns).astype(np.float32),
        np.sin(turns).astype(np.float32),
        np.block([[cosine, -sine], [sine, cosine]]).astype(np.float32),
    )


def body(traces, band_gain, aperture, taper, weights, spread):
    f32 = jnp.float32
    blocks, per_block, samples = traces.shape
    depth = weights.shape[2]
    tile_at = lax.axis_index(TILE)
    sent = pl.pallas_call(
        pack_kernel,
        out_shape=jax.ShapeDtypeStruct((64 * (blocks + 2), LANES), f32),
        in_specs=[SMEM, HBM, HBM, HBM],
        out_specs=VMEM,
        scratch_shapes=[
            pltpu.VMEM((8, blocks * per_block, LANES), f32),
            pltpu.VMEM((4, blocks), jnp.int32),
            pltpu.VMEM((4, blocks), f32),
            pltpu.SemaphoreType.DMA((8,)),
            pltpu.SemaphoreType.DMA((2,)),
        ],
        compiler_params=pltpu.CompilerParams(vmem_limit_bytes=6 * MIB),
        name="pack",
    )(
        ((lax.axis_index(NEAR) - SPREAD_FIRST) % 4).reshape(1),
        in_hbm(traces.reshape(blocks * per_block, samples)),
        in_hbm(aperture.T),
        in_hbm(taper.T),
    )
    got = lax.all_to_all(
        sent.reshape(64, -1, 2, LANES), NEAR, 0, 0, axis_index_groups=[SPREAD_ORDER], tiled=True
    )
    sent = pl.pallas_call(
        stack_kernel,
        out_shape=jax.ShapeDtypeStruct((8 * 33, LANES), f32),
        in_specs=[VMEM],
        out_specs=VMEM,
        compiler_params=pltpu.CompilerParams(vmem_limit_bytes=16 * MIB),
        name="stack",
    )(got.reshape(-1, LANES))
    got = lax.all_to_all(
        sent.reshape(8, 33, 1, LANES), FAR, 0, 0, axis_index_groups=[FAR_ORDER], tiled=True
    )
    sent, counts = pl.pallas_call(
        sum_kernel,
        out_shape=(
            jax.ShapeDtypeStruct((64, LANES), f32),
            jax.ShapeDtypeStruct((1, LANES), f32),
        ),
        in_specs=[VMEM],
        out_specs=(VMEM, VMEM),
        compiler_params=pltpu.CompilerParams(vmem_limit_bytes=2 * MIB),
        name="sum",
    )(got.reshape(-1, LANES))
    got = lax.all_to_all(
        sent.reshape(64, 1, LANES), NEAR, 0, 0, axis_index_groups=[GATHER_ORDER], tiled=True
    )
    image = pl.pallas_call(
        image_kernel,
        out_shape=jax.ShapeDtypeStruct((depth, spread.shape[2]), f32),
        in_specs=[SMEM] + [VMEM] * 8,
        out_specs=VMEM,
        compiler_params=pltpu.CompilerParams(vmem_limit_bytes=16 * MIB),
        name="image",
    )(
        tile_at.reshape(1),
        got.reshape(64, LANES),
        counts,
        band_gain.reshape(LANES, RADIX).T,
        *[jnp.asarray(part) for part in fourier_parts()],
        spread[0],
        weights[0],
    )
    return image[None]


def solution(mesh):
    fine = Mesh(
        mesh.devices.reshape(2, 4, 2, 4, 4, 2),
        ("section", "z_far", "z_pair", "y", "x", "sub"),
    )
    everyone = ("section",) + TILE + ("sub",)
    placed = (
        P(everyone, None, None),
        P(),
        P(everyone, None),
        P(everyone, None),
        P(TILE, None, ("section", "sub")),
        P(TILE, None, None),
    )
    return jax.shard_map(
        body,
        mesh=fine,
        in_specs=placed,
        out_specs=P(TILE, ("section", "sub"), None),
        check_vma=False,
    )
```

```python
import math

import jax
import jax.numpy as jnp
import numpy as np
from jax import lax
from jax.experimental import pallas as pl
from jax.experimental.pallas import tpu as pltpu
from jax.sharding import Mesh
from jax.sharding import PartitionSpec as P

LANES = 128
RADIX = 8
HBM = pl.BlockSpec(memory_space=pl.ANY)
VMEM = pl.BlockSpec(memory_space=pltpu.VMEM)
SMEM = pl.BlockSpec(memory_space=pltpu.SMEM)
NEAR = ("section", "y", "x", "z_pair")
SPREAD_FIRST = 53
GATHER_FIRST = 63
SPREAD_ORDER = [(SPREAD_FIRST + i) % 64 for i in range(64)]
GATHER_ORDER = [(GATHER_FIRST + i) % 64 for i in range(64)]
FAR = ("z_far", "sub")
FAR_ORDER = [3, 2, 1, 0, 5, 4, 7, 6]
TILE = ("z_far", "z_pair", "y", "x")
SIZES = {"section": 2, "z_pair": 2, "y": 4, "x": 4}
MIB = 1 << 20


def halves(value):
    high = value.astype(jnp.bfloat16)
    low = (value - high.astype(jnp.float32)).astype(jnp.bfloat16)
    return high, low


def product(left_high, left_low, right_high, right_low):
    rows = left_high.shape[0]
    both = jnp.dot(
        jnp.concatenate([left_high, left_low], axis=0),
        right_high,
        preferred_element_type=jnp.float32,
    )
    cross = jnp.dot(left_high, right_low, preferred_element_type=jnp.float32)
    return both[:rows] + (both[rows:] + cross)


def in_hbm(array):
    return pltpu.with_memory_space_constraint(array, pltpu.HBM)


def in_vmem(array):
    return pltpu.with_memory_space_constraint(array, pltpu.VMEM)


def pack_kernel(
    place_ref,
    rows_hbm,
    aperture_hbm,
    taper_hbm,
    out_ref,
    columns_ref,
    aperture_ref,
    taper_ref,
    sems,
    list_sems,
):
    blocks = rows_hbm.shape[0] // 8
    copies = [
        pltpu.make_async_copy(aperture_hbm, aperture_ref, list_sems.at[0]),
        pltpu.make_async_copy(taper_hbm, taper_ref, list_sems.at[1]),
    ]
    for copy in copies:
        copy.start()
    for j in range(8):
        copy = pltpu.make_async_copy(
            rows_hbm.at[:, j * LANES : (j + 1) * LANES], columns_ref.at[j], sems.at[j]
        )
        copy.start()
        copies.append(copy)
    copies.pop(0).wait()
    copies.pop(0).wait()
    lists = jnp.concatenate([aperture_ref[...].astype(jnp.float32), taper_ref[...]], axis=0)
    lists = jnp.concatenate([lists] * 4, axis=1)
    entry = lax.broadcasted_iota(jnp.int32, (8, LANES), 0) + place_ref[0]
    lane = lax.broadcasted_iota(jnp.int32, (8, LANES), 1)
    lists = jnp.where(lane // blocks == entry % 4, lists, 0.0)
    lists = jnp.concatenate(
        [jnp.sum(lists[4 * i : 4 * i + 4], axis=0, keepdims=True) for i in range(2)], axis=0
    )
    height = blocks + 2
    for d in range(64):
        out_ref[height * d + blocks : height * (d + 1), :] = lists
    for j in range(8):
        copies[j].wait()
        for r in range(8):
            first = height * SPREAD_ORDER.index(GATHER_ORDER[8 * r + j])
            at = 0
            while at < blocks:
                count = min(8 - (first + at) % 8, blocks - at)
                out_ref[first + at : first + at + count, :] = columns_ref[
                    j, pl.ds(r + 8 * at, count, stride=8), :
                ]
                at += count


def stack_kernel(got_ref, out_ref):
    sources, blocks, tiles = 64, 32, 128
    height = blocks + 2
    tile_ids = lax.broadcasted_iota(jnp.int32, (tiles, LANES), 0).astype(jnp.float32)
    row = lax.broadcasted_iota(jnp.int32, (8, LANES), 0)
    lane = lax.broadcasted_iota(jnp.int32, (8, LANES), 1)
    own = lane // blocks == row % 4

    def entries(offset, first, a):
        rows = got_ref[pl.ds(height * first + offset, 8, stride=height), :]
        rows = rows if a == 0 else pltpu.roll(rows, LANES - blocks * a, axis=1)
        rows = jnp.where(own, rows, 0.0)
        rows = rows + pltpu.roll(rows, 1, axis=0)
        return rows + pltpu.roll(rows, 2, axis=0)

    mixing, named = [], jnp.zeros((tiles, LANES), jnp.float32)
    for first in range(0, sources, 8):
        apertures = [entries(blocks, first, a) for a in range(4)]
        tapers = [entries(blocks + 1, first, a) for a in range(4)]
        for at in (3, 7):
            mix = jnp.zeros((tiles, LANES), jnp.float32)
            for a in range(4):
                hit = apertures[a][at : at + 1, :] == tile_ids
                mix = jnp.where(hit, tapers[a][at : at + 1, :], mix)
            mixing.append(mix)
            named = named + jnp.where(mix > 0.0, 1.0, 0.0)
    mix_high, mix_low = halves(jnp.concatenate(mixing, axis=1))
    samples = jnp.concatenate(
        [got_ref[height * s : height * s + blocks, :] for s in range(sources)], axis=0
    )
    stacked = product(mix_high, mix_low, *halves(samples))
    counts = lax.dot_general(
        jnp.ones((8, LANES), jnp.bfloat16),
        named.astype(jnp.bfloat16),
        (((1,), (1,)), ((), ())),
        preferred_element_type=jnp.float32,
    )
    for p in range(8):
        first = (FAR_ORDER[p] // 2) * 32
        out_ref[33 * p : 33 * p + 32, :] = stacked[first : first + 32]
        out_ref[33 * p + 32 : 33 * p + 33, :] = counts[:1]


def near_tiles():
    owners = []
    places = list(np.ndindex(*[SIZES[axis] for axis in NEAR]))
    for index in GATHER_ORDER:
        at = dict(zip(NEAR, places[index]))
        owners.append((at["z_pair"] * 4 + at["y"]) * 4 + at["x"])
    return owners


def sum_kernel(got_ref, out_ref, counts_ref):
    total, counts = got_ref[:32, :], got_ref[32:33, :]
    for p in range(1, 8):
        total = total + got_ref[33 * p : 33 * p + 32, :]
        counts = counts + got_ref[33 * p + 32 : 33 * p + 33, :]
    for d, owner in enumerate(near_tiles()):
        out_ref[d : d + 1, :] = total[owner : owner + 1]
    counts_ref[...] = counts


def image_kernel(
    tile_ref,
    stacked_ref,
    counts_ref,
    gain_ref,
    turn_cos_ref,
    turn_sin_ref,
    table_ref,
    spread_ref,
    weights_ref,
    out_ref,
):
    samples = RADIX * LANES
    parts = [stacked_ref[pl.ds(j, 8, stride=RADIX), :] for j in range(RADIX)]
    angle = [2.0 * math.pi * j / RADIX for j in range(RADIX)]

    def weighted(terms, factors):
        total = None
        for term, factor in zip(terms, factors):
            if abs(factor) < 1e-9:
                continue
            if abs(factor - 1.0) < 1e-9:
                piece = term
            elif abs(factor + 1.0) < 1e-9:
                piece = -term
            else:
                piece = term * np.float32(factor)
            total = piece if total is None else total + piece
        return jnp.zeros_like(terms[0]) if total is None else total

    real_rows, imag_rows = [], []
    for k in range(RADIX):
        real = weighted(parts, [math.cos(angle[j * k % RADIX]) for j in range(RADIX)])
        imag = weighted(parts, [-math.sin(angle[j * k % RADIX]) for j in range(RADIX)])
        turn_cos = turn_cos_ref[k : k + 1, :]
        turn_sin = turn_sin_ref[k : k + 1, :]
        real_rows.append(real * turn_cos + imag * turn_sin)
        imag_rows.append(imag * turn_cos - real * turn_sin)
    waves = jnp.concatenate(
        [jnp.concatenate(real_rows, axis=0), jnp.concatenate(imag_rows, axis=0)], axis=1
    )
    ahead = halves(table_ref[...])
    back = []
    for part in ahead:
        top = jnp.concatenate([part[:LANES, :LANES], part[LANES:, :LANES]], axis=1)
        bottom = jnp.concatenate([part[:LANES, LANES:], part[LANES:, LANES:]], axis=1)
        back.append(jnp.concatenate([top, bottom], axis=0))
    spectra = product(*halves(waves), *ahead)
    gains = jnp.concatenate(
        [jnp.broadcast_to(gain_ref[k : k + 1, :], (8, LANES)) for k in range(RADIX)], axis=0
    )
    spectra = spectra * jnp.concatenate([gains, gains], axis=1)
    waves = product(*halves(spectra), *back)
    real_rows, imag_rows = [], []
    for k in range(RADIX):
        real = waves[8 * k : 8 * k + 8, :LANES]
        imag = waves[8 * k : 8 * k + 8, LANES:]
        turn_cos = turn_cos_ref[k : k + 1, :]
        turn_sin = turn_sin_ref[k : k + 1, :]
        real_rows.append(real * turn_cos - imag * turn_sin)
        imag_rows.append(imag * turn_cos + real * turn_sin)
    filtered = []
    for j in range(RADIX):
        filtered.append(
            weighted(
                real_rows + imag_rows,
                [math.cos(angle[j * k % RADIX]) for k in range(RADIX)]
                + [-math.sin(angle[j * k % RADIX]) for k in range(RADIX)],
            )
            * np.float32(1.0 / samples)
        )
    filtered = jnp.concatenate(filtered, axis=1)
    lane = lax.broadcasted_iota(jnp.int32, (1, LANES), 1)
    fold = jnp.sum(
        jnp.where(lane == tile_ref[0], counts_ref[0:1, :], 0.0), axis=1, keepdims=True
    )
    focused = product(*halves(filtered), *halves(weights_ref[...])) / jnp.sqrt(fold)
    focused_high, focused_low = halves(focused)
    spread_high, spread_low = halves(spread_ref[...])
    out_ref[...] = lax.dot_general(
        jnp.concatenate([focused_high, focused_high, focused_low], axis=0),
        jnp.concatenate([spread_high, spread_low, spread_high], axis=0),
        (((0,), (0,)), ((), ())),
        preferred_element_type=jnp.float32,
    )


def fourier_parts():
    lane = np.arange(LANES)
    turns = 2.0 * np.pi * np.arange(RADIX)[:, None] * lane[None, :] / (RADIX * LANES)
    angles = 2.0 * np.pi * (lane[:, None] * lane[None, :] % LANES) / LANES
    cosine, sine = np.cos(angles), np.sin(angles)
    return (
        np.cos(turns).astype(np.float32),
        np.sin(turns).astype(np.float32),
        np.block([[cosine, -sine], [sine, cosine]]).astype(np.float32),
    )


def body(traces, band_gain, aperture, taper, weights, spread):
    f32 = jnp.float32
    blocks, per_block, samples = traces.shape
    depth = weights.shape[2]
    tile_at = lax.axis_index(TILE)
    sent = pl.pallas_call(
        pack_kernel,
        out_shape=jax.ShapeDtypeStruct((64 * (blocks + 2), LANES), f32),
        in_specs=[SMEM, HBM, HBM, HBM],
        out_specs=VMEM,
        scratch_shapes=[
            pltpu.VMEM((8, blocks * per_block, LANES), f32),
            pltpu.VMEM((4, blocks), jnp.int32),
            pltpu.VMEM((4, blocks), f32),
            pltpu.SemaphoreType.DMA((8,)),
            pltpu.SemaphoreType.DMA((2,)),
        ],
        compiler_params=pltpu.CompilerParams(vmem_limit_bytes=6 * MIB),
        name="pack",
    )(
        ((lax.axis_index(NEAR) - SPREAD_FIRST) % 4).reshape(1),
        in_hbm(traces.reshape(blocks * per_block, samples)),
        in_hbm(aperture.T),
        in_hbm(taper.T),
    )
    got = lax.all_to_all(
        sent.reshape(64, -1, 2, LANES), NEAR, 0, 0, axis_index_groups=[SPREAD_ORDER], tiled=True
    )
    sent = pl.pallas_call(
        stack_kernel,
        out_shape=jax.ShapeDtypeStruct((8 * 33, LANES), f32),
        in_specs=[VMEM],
        out_specs=VMEM,
        compiler_params=pltpu.CompilerParams(vmem_limit_bytes=16 * MIB),
        name="stack",
    )(got.reshape(-1, LANES))
    got = lax.all_to_all(
        sent.reshape(8, 33, 1, LANES), FAR, 0, 0, axis_index_groups=[FAR_ORDER], tiled=True
    )
    sent, counts = pl.pallas_call(
        sum_kernel,
        out_shape=(
            jax.ShapeDtypeStruct((64, LANES), f32),
            jax.ShapeDtypeStruct((1, LANES), f32),
        ),
        in_specs=[VMEM],
        out_specs=(VMEM, VMEM),
        compiler_params=pltpu.CompilerParams(vmem_limit_bytes=2 * MIB),
        name="sum",
    )(got.reshape(-1, LANES))
    got = lax.all_to_all(
        sent.reshape(64, 1, LANES), NEAR, 0, 0, axis_index_groups=[GATHER_ORDER], tiled=True
    )
    image = pl.pallas_call(
        image_kernel,
        out_shape=jax.ShapeDtypeStruct((depth, spread.shape[2]), f32),
        in_specs=[SMEM] + [VMEM] * 8,
        out_specs=VMEM,
        compiler_params=pltpu.CompilerParams(vmem_limit_bytes=16 * MIB),
        name="image",
    )(
        tile_at.reshape(1),
        got.reshape(64, LANES),
        counts,
        band_gain.reshape(LANES, RADIX).T,
        *[jnp.asarray(part) for part in fourier_parts()],
        spread[0],
        weights[0],
    )
    return image[None]


def solution(mesh):
    fine = Mesh(
        mesh.devices.reshape(2, 4, 2, 4, 4, 2),
        ("section", "z_far", "z_pair", "y", "x", "sub"),
    )
    everyone = ("section",) + TILE + ("sub",)
    placed = (
        P(everyone, None, None),
        P(),
        P(everyone, None),
        P(everyone, None),
        P(TILE, None, ("section", "sub")),
        P(TILE, None, None),
    )
    return jax.shard_map(
        body,
        mesh=fine,
        in_specs=placed,
        out_specs=P(TILE, ("section", "sub"), None),
        check_vma=False,
    )
```

```python
import math

import jax
import jax.numpy as jnp
import numpy as np
from jax import lax
from jax.experimental import pallas as pl
from jax.experimental.pallas import tpu as pltpu
from jax.sharding import Mesh
from jax.sharding import PartitionSpec as P

LANES = 128
RADIX = 8
HBM = pl.BlockSpec(memory_space=pl.ANY)
VMEM = pl.BlockSpec(memory_space=pltpu.VMEM)
SMEM = pl.BlockSpec(memory_space=pltpu.SMEM)
NEAR = ("section", "y", "x", "z_pair")
SPREAD_FIRST = 53
GATHER_FIRST = 63
SPREAD_ORDER = [(SPREAD_FIRST + i) % 64 for i in range(64)]
GATHER_ORDER = [(GATHER_FIRST + i) % 64 for i in range(64)]
FAR = ("z_far", "sub")
FAR_ORDER = [3, 2, 1, 0, 5, 4, 7, 6]
TILE = ("z_far", "z_pair", "y", "x")
SIZES = {"section": 2, "z_pair": 2, "y": 4, "x": 4}
MIB = 1 << 20


def halves(value):
    high = value.astype(jnp.bfloat16)
    low = (value - high.astype(jnp.float32)).astype(jnp.bfloat16)
    return high, low


def product(left_high, left_low, right_high, right_low):
    rows = left_high.shape[0]
    both = jnp.dot(
        jnp.concatenate([left_high, left_low], axis=0),
        right_high,
        preferred_element_type=jnp.float32,
    )
    cross = jnp.dot(left_high, right_low, preferred_element_type=jnp.float32)
    return both[:rows] + (both[rows:] + cross)


def in_hbm(array):
    return pltpu.with_memory_space_constraint(array, pltpu.HBM)


def in_vmem(array):
    return pltpu.with_memory_space_constraint(array, pltpu.VMEM)


def pack_kernel(
    place_ref,
    rows_hbm,
    aperture_hbm,
    taper_hbm,
    out_ref,
    columns_ref,
    aperture_ref,
    taper_ref,
    sems,
    list_sems,
):
    blocks = rows_hbm.shape[0] // 8
    copies = [
        pltpu.make_async_copy(aperture_hbm, aperture_ref, list_sems.at[0]),
        pltpu.make_async_copy(taper_hbm, taper_ref, list_sems.at[1]),
    ]
    for copy in copies:
        copy.start()
    for j in range(8):
        copy = pltpu.make_async_copy(
            rows_hbm.at[:, j * LANES : (j + 1) * LANES], columns_ref.at[j], sems.at[j]
        )
        copy.start()
        copies.append(copy)
    copies.pop(0).wait()
    copies.pop(0).wait()
    lists = jnp.concatenate([aperture_ref[...].astype(jnp.float32), taper_ref[...]], axis=0)
    lists = jnp.concatenate([lists] * 4, axis=1)
    entry = lax.broadcasted_iota(jnp.int32, (8, LANES), 0) + place_ref[0]
    lane = lax.broadcasted_iota(jnp.int32, (8, LANES), 1)
    lists = jnp.where(lane // blocks == entry % 4, lists, 0.0)
    lists = jnp.concatenate(
        [jnp.sum(lists[4 * i : 4 * i + 4], axis=0, keepdims=True) for i in range(2)], axis=0
    )
    height = blocks + 2
    for d in range(64):
        out_ref[height * d + blocks : height * (d + 1), :] = lists
    for j in range(8):
        copies[j].wait()
        for r in range(8):
            first = height * SPREAD_ORDER.index(GATHER_ORDER[8 * r + j])
            at = 0
            while at < blocks:
                count = min(8 - (first + at) % 8, blocks - at)
                out_ref[first + at : first + at + count, :] = columns_ref[
                    j, pl.ds(r + 8 * at, count, stride=8), :
                ]
                at += count


def stack_kernel(got_ref, out_ref):
    sources, blocks, tiles = 64, 32, 128
    height = blocks + 2
    tile_ids = lax.broadcasted_iota(jnp.int32, (tiles, LANES), 0).astype(jnp.float32)
    row = lax.broadcasted_iota(jnp.int32, (8, LANES), 0)
    lane = lax.broadcasted_iota(jnp.int32, (8, LANES), 1)
    own = lane // blocks == row % 4

    def entries(offset, first, a):
        rows = got_ref[pl.ds(height * first + offset, 8, stride=height), :]
        rows = rows if a == 0 else pltpu.roll(rows, LANES - blocks * a, axis=1)
        rows = jnp.where(own, rows, 0.0)
        rows = rows + pltpu.roll(rows, 1, axis=0)
        return rows + pltpu.roll(rows, 2, axis=0)

    mixing, named = [], jnp.zeros((tiles, LANES), jnp.float32)
    for first in range(0, sources, 8):
        apertures = [entries(blocks, first, a) for a in range(4)]
        tapers = [entries(blocks + 1, first, a) for a in range(4)]
        for at in (3, 7):
            mix = jnp.zeros((tiles, LANES), jnp.float32)
            for a in range(4):
                hit = apertures[a][at : at + 1, :] == tile_ids
                mix = jnp.where(hit, tapers[a][at : at + 1, :], mix)
            mixing.append(mix)
            named = named + jnp.where(mix > 0.0, 1.0, 0.0)
    mix_high, mix_low = halves(jnp.concatenate(mixing, axis=1))
    samples = jnp.concatenate(
        [got_ref[height * s : height * s + blocks, :] for s in range(sources)], axis=0
    )
    stacked = product(mix_high, mix_low, *halves(samples))
    counts = lax.dot_general(
        jnp.ones((8, LANES), jnp.bfloat16),
        named.astype(jnp.bfloat16),
        (((1,), (1,)), ((), ())),
        preferred_element_type=jnp.float32,
    )
    for p in range(8):
        first = (FAR_ORDER[p] // 2) * 32
        out_ref[33 * p : 33 * p + 32, :] = stacked[first : first + 32]
        out_ref[33 * p + 32 : 33 * p + 33, :] = counts[:1]


def near_tiles():
    owners = []
    places = list(np.ndindex(*[SIZES[axis] for axis in NEAR]))
    for index in GATHER_ORDER:
        at = dict(zip(NEAR, places[index]))
        owners.append((at["z_pair"] * 4 + at["y"]) * 4 + at["x"])
    return owners


def sum_kernel(got_ref, out_ref, counts_ref):
    total, counts = got_ref[:32, :], got_ref[32:33, :]
    for p in range(1, 8):
        total = total + got_ref[33 * p : 33 * p + 32, :]
        counts = counts + got_ref[33 * p + 32 : 33 * p + 33, :]
    for d, owner in enumerate(near_tiles()):
        out_ref[d : d + 1, :] = total[owner : owner + 1]
    counts_ref[...] = counts


def image_kernel(
    tile_ref,
    stacked_ref,
    counts_ref,
    gain_ref,
    turn_cos_ref,
    turn_sin_ref,
    table_ref,
    spread_ref,
    weights_ref,
    out_hbm,
    slab_ref,
    sems,
):
    samples = RADIX * LANES
    parts = [stacked_ref[pl.ds(j, 8, stride=RADIX), :] for j in range(RADIX)]
    angle = [2.0 * math.pi * j / RADIX for j in range(RADIX)]

    def weighted(terms, factors):
        total = None
        for term, factor in zip(terms, factors):
            if abs(factor) < 1e-9:
                continue
            if abs(factor - 1.0) < 1e-9:
                piece = term
            elif abs(factor + 1.0) < 1e-9:
                piece = -term
            else:
                piece = term * np.float32(factor)
            total = piece if total is None else total + piece
        return jnp.zeros_like(terms[0]) if total is None else total

    real_rows, imag_rows = [], []
    for k in range(RADIX):
        real = weighted(parts, [math.cos(angle[j * k % RADIX]) for j in range(RADIX)])
        imag = weighted(parts, [-math.sin(angle[j * k % RADIX]) for j in range(RADIX)])
        turn_cos = turn_cos_ref[k : k + 1, :]
        turn_sin = turn_sin_ref[k : k + 1, :]
        real_rows.append(real * turn_cos + imag * turn_sin)
        imag_rows.append(imag * turn_cos - real * turn_sin)
    waves = jnp.concatenate(
        [jnp.concatenate(real_rows, axis=0), jnp.concatenate(imag_rows, axis=0)], axis=1
    )
    ahead = halves(table_ref[...])
    back = []
    for part in ahead:
        top = jnp.concatenate([part[:LANES, :LANES], part[LANES:, :LANES]], axis=1)
        bottom = jnp.concatenate([part[:LANES, LANES:], part[LANES:, LANES:]], axis=1)
        back.append(jnp.concatenate([top, bottom], axis=0))
    spectra = product(*halves(waves), *ahead)
    gains = jnp.concatenate(
        [jnp.broadcast_to(gain_ref[k : k + 1, :], (8, LANES)) for k in range(RADIX)], axis=0
    )
    spectra = spectra * jnp.concatenate([gains, gains], axis=1)
    waves = product(*halves(spectra), *back)
    real_rows, imag_rows = [], []
    for k in range(RADIX):
        real = waves[8 * k : 8 * k + 8, :LANES]
        imag = waves[8 * k : 8 * k + 8, LANES:]
        turn_cos = turn_cos_ref[k : k + 1, :]
        turn_sin = turn_sin_ref[k : k + 1, :]
        real_rows.append(real * turn_cos - imag * turn_sin)
        imag_rows.append(imag * turn_cos + real * turn_sin)
    filtered = []
    for j in range(RADIX):
        filtered.append(
            weighted(
                real_rows + imag_rows,
                [math.cos(angle[j * k % RADIX]) for k in range(RADIX)]
                + [-math.sin(angle[j * k % RADIX]) for k in range(RADIX)],
            )
            * np.float32(1.0 / samples)
        )
    filtered = jnp.concatenate(filtered, axis=1)
    lane = lax.broadcasted_iota(jnp.int32, (1, LANES), 1)
    fold = jnp.sum(
        jnp.where(lane == tile_ref[0], counts_ref[0:1, :], 0.0), axis=1, keepdims=True
    )
    filtered = halves(filtered)
    spread_high, spread_low = halves(spread_ref[...])
    spread = jnp.concatenate([spread_high, spread_low, spread_high], axis=0)
    copies = []
    for i, (low, high) in enumerate(((0, 256), (256, out_hbm.shape[0]))):
        focused = product(*filtered, *halves(weights_ref[:, low:high])) / jnp.sqrt(fold)
        focused_high, focused_low = halves(focused)
        slab_ref[low:high, :] = lax.dot_general(
            jnp.concatenate([focused_high, focused_high, focused_low], axis=0),
            spread,
            (((0,), (0,)), ((), ())),
            preferred_element_type=jnp.float32,
        )
        copy = pltpu.make_async_copy(slab_ref.at[low:high], out_hbm.at[low:high], sems.at[i])
        copy.start()
        copies.append(copy)
    for copy in copies:
        copy.wait()


def fourier_parts():
    lane = np.arange(LANES)
    turns = 2.0 * np.pi * np.arange(RADIX)[:, None] * lane[None, :] / (RADIX * LANES)
    angles = 2.0 * np.pi * (lane[:, None] * lane[None, :] % LANES) / LANES
    cosine, sine = np.cos(angles), np.sin(angles)
    return (
        np.cos(turns).astype(np.float32),
        np.sin(turns).astype(np.float32),
        np.block([[cosine, -sine], [sine, cosine]]).astype(np.float32),
    )


def body(traces, band_gain, aperture, taper, weights, spread):
    f32 = jnp.float32
    blocks, per_block, samples = traces.shape
    depth = weights.shape[2]
    tile_at = lax.axis_index(TILE)
    sent = pl.pallas_call(
        pack_kernel,
        out_shape=jax.ShapeDtypeStruct((64 * (blocks + 2), LANES), f32),
        in_specs=[SMEM, HBM, HBM, HBM],
        out_specs=VMEM,
        scratch_shapes=[
            pltpu.VMEM((8, blocks * per_block, LANES), f32),
            pltpu.VMEM((4, blocks), jnp.int32),
            pltpu.VMEM((4, blocks), f32),
            pltpu.SemaphoreType.DMA((8,)),
            pltpu.SemaphoreType.DMA((2,)),
        ],
        compiler_params=pltpu.CompilerParams(vmem_limit_bytes=6 * MIB),
        name="pack",
    )(
        ((lax.axis_index(NEAR) - SPREAD_FIRST) % 4).reshape(1),
        in_hbm(traces.reshape(blocks * per_block, samples)),
        in_hbm(aperture.T),
        in_hbm(taper.T),
    )
    got = lax.all_to_all(
        sent.reshape(64, -1, 2, LANES), NEAR, 0, 0, axis_index_groups=[SPREAD_ORDER], tiled=True
    )
    sent = pl.pallas_call(
        stack_kernel,
        out_shape=jax.ShapeDtypeStruct((8 * 33, LANES), f32),
        in_specs=[VMEM],
        out_specs=VMEM,
        compiler_params=pltpu.CompilerParams(vmem_limit_bytes=16 * MIB),
        name="stack",
    )(got.reshape(-1, LANES))
    got = lax.all_to_all(
        sent.reshape(8, 33, 1, LANES), FAR, 0, 0, axis_index_groups=[FAR_ORDER], tiled=True
    )
    sent, counts = pl.pallas_call(
        sum_kernel,
        out_shape=(
            jax.ShapeDtypeStruct((64, LANES), f32),
            jax.ShapeDtypeStruct((1, LANES), f32),
        ),
        in_specs=[VMEM],
        out_specs=(VMEM, VMEM),
        compiler_params=pltpu.CompilerParams(vmem_limit_bytes=2 * MIB),
        name="sum",
    )(got.reshape(-1, LANES))
    got = lax.all_to_all(
        sent.reshape(64, 1, LANES), NEAR, 0, 0, axis_index_groups=[GATHER_ORDER], tiled=True
    )
    image = pl.pallas_call(
        image_kernel,
        out_shape=jax.ShapeDtypeStruct((depth, spread.shape[2]), f32),
        in_specs=[SMEM] + [VMEM] * 8,
        out_specs=HBM,
        scratch_shapes=[
            pltpu.VMEM((depth, spread.shape[2]), f32),
            pltpu.SemaphoreType.DMA((2,)),
        ],
        compiler_params=pltpu.CompilerParams(vmem_limit_bytes=16 * MIB),
        name="image",
    )(
        tile_at.reshape(1),
        got.reshape(64, LANES),
        counts,
        band_gain.reshape(LANES, RADIX).T,
        *[jnp.asarray(part) for part in fourier_parts()],
        spread[0],
        weights[0],
    )
    return image[None]


def solution(mesh):
    fine = Mesh(
        mesh.devices.reshape(2, 4, 2, 4, 4, 2),
        ("section", "z_far", "z_pair", "y", "x", "sub"),
    )
    everyone = ("section",) + TILE + ("sub",)
    placed = (
        P(everyone, None, None),
        P(),
        P(everyone, None),
        P(everyone, None),
        P(TILE, None, ("section", "sub")),
        P(TILE, None, None),
    )
    return jax.shard_map(
        body,
        mesh=fine,
        in_specs=placed,
        out_specs=P(TILE, ("section", "sub"), None),
        check_vma=False,
    )
```
